32 devices in a mesh: pb: 4 (over y, x), ka: 8 (over z, core).
Axes of the slice: x: 2, y: 2, z: 4, core: 2. Of those that a mesh axis runs over, the one named last changes fastest.
Arguments:
- envelopes: bfloat16 [256, 36864], P('ka'), may hold values from -6 to 6
- coupling: bfloat16 [8, 9, 32, 2304], P('pb', None, None, 'ka'), may hold values from -3 to 3
- kq_map: int32 [8, 2304], P('pb', 'ka'), may hold values from 0 to 2303, as said below
Outputs:
- exciton_coupling: float32 [8, 9, 256, 256], P('pb', None, 'ka')
The draws below stay inside these ranges and needn't reach their ends.
Inputs may be any that keep to these rules, and one draw needn't show every extreme that they name: `kq_map`: each row q is a lattice translation: k = kx * 96 + ky goes to ((kx + a_q) mod 24) * 96 + (ky + b_q) mod 96, with -3 <= a_q <= 3; a_q = 3 and a_q = -3 both occur.
All inputs are finite; a program needn't handle non-finite values.
Results may differ from the reference program's by a relative error of at most 0.0029.
Values may be sent and summed in bfloat16 or wider, within the bound.
No kernel may reach another device: no remote copies, remote signals or barrier semaphores. Data moves between devices by JAX's collectives and lax.ppermute only.
A program may use at most 64 MiB of HBM per device.

```python
import math
import jax
import jax.numpy as jnp
from jax import lax

S = 256
NU = 9
KY = 96
KXL = 3
KX = 24
Q = 8


def draw_kq_map(key, part):
    key_x, key_y = jax.random.split(jax.random.fold_in(key, 11))
    shift_x = jax.random.randint(key_x, (Q,), -KXL, KXL + 1)
    shift_x = shift_x.at[0].set(KXL).at[1].set(-KXL)
    shift_y = jax.random.randint(key_y, (Q,), 0, KY)
    index = jnp.arange(KX * KY, dtype=jnp.int32)
    line_x = index // KY
    line_y = index % KY
    target_x = (line_x[None, :] + shift_x[:, None]) % KX
    target_y = (line_y[None, :] + shift_y[:, None]) % KY
    return (target_x * KY + target_y).astype(jnp.int32)


def block_scale(own_key, dims, cuts, smallest, largest):
    loudness, own = 1.0, jax.random.fold_in(own_key, 6)
    for dim, parts in cuts:
        heights = jnp.exp(jax.random.uniform(jax.random.fold_in(own, dim), (parts,), jnp.float32, smallest / len(cuts), largest / len(cuts)))
        loudness = loudness * jnp.repeat(heights, dims[dim] // parts).reshape([-1 if axis == dim else 1 for axis in range(len(dims))])
    return loudness


def normal_values(stream_key, shape, spread, reach, cuts=(), kind=jnp.bfloat16):
    factor_of = block_scale(stream_key, shape, cuts, -0.22, 0.18) if cuts else 1.0
    values = jax.random.normal(stream_key, shape, jnp.float32) * spread * factor_of
    return jnp.minimum(jnp.maximum(values, -reach), reach).astype(kind)


def setup_inputs(seed: int = 0) -> dict:
    arg_keys = jax.random.split(jax.random.key(seed), 4)
    return {
        "envelopes": normal_values(arg_keys[0], (S, KX * KY * 16), 1.0, 6.0, ((0, 8),)),
        "coupling": normal_values(arg_keys[1], (Q, NU, 32, KX * KY), 4 ** -0.5, 3.0, ((0, 4), (3, 8))),
        "kq_map": draw_kq_map(jax.random.fold_in(arg_keys[3], 71), 0),
    }


def reference(envelopes, coupling, kq_map):
    total_k = KX * KY
    amps_f = envelopes.reshape(S, total_k, 4, 4).astype(jnp.float32)
    flat = envelopes.reshape(S, total_k, 16)
    factor = 1.0 / math.sqrt(16.0 * total_k)

    def per_q(qidx):
        shifted = jnp.take(flat, kq_map[qidx], axis=1).reshape(S, total_k * 16)

        def per_mode(mode):
            table = coupling[qidx, mode].astype(jnp.float32)
            g_cond = table[:16].reshape(4, 4, total_k)
            g_val = table[16:].reshape(4, 4, total_k)
            elec = jnp.einsum('dck,skvc->skvd', g_cond, amps_f)
            hole = jnp.einsum('vwk,skvc->skwc', g_val, amps_f)
            diff = (elec - hole).astype(jnp.bfloat16).reshape(S, total_k * 16)
            return jnp.dot(shifted, diff.T, preferred_element_type=jnp.float32)
        return lax.map(per_mode, jnp.arange(NU, dtype=jnp.int32))
    return lax.map(per_q, jnp.arange(Q, dtype=jnp.int32)) * factor
```

```python
import functools
import math

import jax
import jax.numpy as jnp
from jax import lax
from jax.experimental import pallas as pl
from jax.experimental.pallas import tpu as pltpu
from jax.sharding import PartitionSpec as P

KY = 96
BANDS = 16
LINE = KY * BANDS
GROUPS = 3
F32 = jnp.float32
BF16 = jnp.bfloat16


def contract(a, b, dim_a, dim_b):
    return lax.dot_general(a, b, (((dim_a,), (dim_b,)), ((), ())), preferred_element_type=F32)


def prep_kernel(pieces, block, lines, scalars, *refs):
    ins, (own_ref, shift_ref, window, sems) = refs[: 2 * pieces], refs[2 * pieces :]
    start_line, roll, core, pb = scalars[0], scalars[1], scalars[2], scalars[3]
    rows = ins[0].shape[0]
    copies = []
    for half in range(2):
        for index in range(pieces):
            src = ins[half * pieces + index]
            size = src.shape[1]
            offset = 0
            if pieces > 1:
                turn = core if half == 0 else 1 - core
                rel = (0, 1 + turn, 2 - turn, 3)[index]
                offset = pl.multiple_of((pb ^ rel) * block, 128)
            copy = pltpu.make_async_copy(src, window.at[half, :, pl.ds(offset, size)], sems.at[half, index])
            copy.start()
            copies.append(copy)
    for copy in copies:
        copy.wait()
    first = core == 0

    def both(lane):
        mine = window[0, :, pl.ds(pl.multiple_of(lane, 128), LINE)].astype(F32)
        other = window[1, :, pl.ds(pl.multiple_of(lane, 128), LINE)].astype(F32)
        return jnp.concatenate([jnp.where(first, mine, other), jnp.where(first, other, mine)], axis=0)

    for line in range(lines):
        to = slice(line * LINE, (line + 1) * LINE)
        own_ref[:, to] = both((lines // 2 + line) * LINE).astype(BF16)
        shifted = both((start_line + line) * LINE)
        shift_ref[:, to] = pltpu.roll(shifted, roll, 1).astype(BF16)


def prepare(scalars, mine, other, block, lines):
    rows = mine[0].shape[0]
    pieces = len(mine)
    out = jax.ShapeDtypeStruct((2 * rows, lines * LINE), BF16)
    return pl.pallas_call(
        functools.partial(prep_kernel, pieces, block, lines),
        in_specs=[pl.BlockSpec(memory_space=pltpu.SMEM)] + [pl.BlockSpec(memory_space=pl.ANY)] * (2 * pieces),
        out_specs=[pl.BlockSpec(memory_space=pltpu.VMEM)] * 2,
        out_shape=[out, out],
        scratch_shapes=[
            pltpu.VMEM((2, rows, 2 * lines * LINE), BF16),
            pltpu.SemaphoreType.DMA((2, pieces)),
        ],
        compiler_params=pltpu.CompilerParams(vmem_limit_bytes=24 << 20),
        name="prepare",
    )(scalars, *mine, *other)


def main_kernel(n_z, factor, scalars, x_ref, mask_ref, *refs):
    owns, shifts = refs[:n_z], refs[n_z : 2 * n_z]
    mine_ref, sends, total = refs[2 * n_z], refs[2 * n_z + 1 : -1], refs[-1]
    step = pl.program_id(0)
    branches = x_ref.shape[0]

    @pl.when(step == 0)
    def _():
        total[...] = jnp.zeros_like(total)

    for branch in range(branches):
        parts = []
        for tile in range(LINE // 256):
            lanes = slice(tile * 256, (tile + 1) * 256)
            matrix = jnp.concatenate([x_ref[branch, :, lanes]] * 16, axis=0) * mask_ref[...]
            amps = jnp.concatenate([ref[:, lanes] for ref in owns], axis=0)
            parts.append(contract(amps, matrix, 1, 0).astype(BF16))
        diff = jnp.concatenate(parts, axis=1)
        shifted = jnp.concatenate([ref[...] for ref in shifts], axis=0)
        total[branch] += contract(shifted, diff, 1, 1)

    @pl.when(step == pl.num_programs(0) - 1)
    def _():
        core, roll = scalars[0], scalars[1]
        rows = mine_ref.shape[1]
        index = 0
        for chip in range(n_z):
            for flip in range(2):
                at = pl.multiple_of(chip * 2 * rows + rows * (core ^ flip), rows)
                for branch in range(branches):
                    piece = pltpu.roll(total[branch, pl.ds(at, rows), :] * factor, roll, 1)
                    if chip == 0 and flip == 0:
                        mine_ref[branch] = piece
                    else:
                        sends[index][branch] = piece.astype(BF16)
                if chip or flip:
                    index += 1


def products(scalars, x, mask, owns, shifts, rows, factor):
    n_z = len(owns)
    branches = x.shape[0]
    states = 2 * n_z * rows
    lines = x.shape[2] // LINE
    by_line = pl.BlockSpec((2 * rows, LINE), lambda i: (0, i))
    piece = pl.BlockSpec((branches, rows, states), lambda i: (0, 0, 0))
    sends = 2 * n_z - 1
    return pl.pallas_call(
        functools.partial(main_kernel, n_z, factor),
        grid=(lines,),
        in_specs=[
            pl.BlockSpec(memory_space=pltpu.SMEM),
            pl.BlockSpec((branches, BANDS, LINE), lambda i: (0, 0, i)),
            pl.BlockSpec((256, 256), lambda i: (0, 0)),
        ]
        + [by_line] * (2 * n_z),
        out_specs=[piece] * (1 + sends),
        out_shape=[jax.ShapeDtypeStruct((branches, rows, states), F32)]
        + [jax.ShapeDtypeStruct((branches, rows, states), BF16)] * sends,
        scratch_shapes=[pltpu.VMEM((branches, states, states), F32)],
        compiler_params=pltpu.CompilerParams(vmem_limit_bytes=40 << 20),
        cost_estimate=pl.CostEstimate(
            flops=4 * branches * states * states * lines * LINE,
            bytes_accessed=4 * states * lines * LINE,
            transcendentals=0,
        ),
        name="products",
    )(scalars, x, mask, *owns, *shifts)


def band_matrices(table):
    branches, _, count = table.shape
    table = table.astype(F32)
    cond = table[:, :16].reshape(branches, 4, 4, count)
    val = table[:, 16:].reshape(branches, 4, 4, count)
    eye = jnp.eye(4, dtype=F32)
    cond = jnp.swapaxes(cond, 1, 2)[:, None, :, None] * eye[None, :, None, :, None, None]
    val = val[:, :, None, :, None] * eye[None, None, :, None, :, None]
    x = (cond - val).astype(BF16).reshape(branches, 16, 16, count)
    return jnp.swapaxes(x, 2, 3).reshape(branches, 16, count * 16)


def shards(envelopes, coupling, kq_map):
    n_pb, n_ka = lax.axis_size("pb"), lax.axis_size("ka")
    assert n_pb == 4 and n_ka % 2 == 0 and coupling.shape[0] == 2
    n_z = n_ka // 2
    rows, width = envelopes.shape
    block = width // n_ka
    block_lines = block // LINE
    lines = 2 * block_lines
    pb, ka = lax.axis_index("pb"), lax.axis_index("ka")
    z, core = ka // 2, ka % 2

    def permute(x, to):
        pairs = []
        for p in range(n_pb):
            for k in range(n_ka):
                tp, tz, tc = to(p, k // 2, k % 2)
                pairs.append((p * n_ka + k, tp * n_ka + (tz % n_z) * 2 + tc))
        return lax.ppermute(x, ("pb", "ka"), pairs)

    def sibling(x):
        return permute(x, lambda p, zz, c: (p, zz, 1 - c))

    def own_block(index):
        return lax.dynamic_slice_in_dim(envelopes, (index % n_ka) * block, block, axis=1)

    window = jnp.concatenate([own_block(2 * z - 1 + w + n_ka) for w in range(4)], axis=1)
    window_other = sibling(window)
    arrived = []
    for e in range(1, n_z):
        piece = own_block(2 * (z - e) - 1 + pb + 2 * n_ka)
        arrived.append(permute(piece, lambda p, zz, c: (p, zz - e, c)))

    first = jnp.where(core == 0, 1, 2)
    table = lax.dynamic_index_in_dim(coupling, core, 0, keepdims=False)
    table_other = sibling(lax.dynamic_index_in_dim(coupling, 1 - core, 0, keepdims=False))
    table = jnp.where(
        core == 0,
        jnp.concatenate([table, table_other], axis=2),
        jnp.concatenate([table_other, table], axis=2),
    )
    x = band_matrices(table)

    origin = lax.dynamic_slice(kq_map, (core, 0), (1, 1))[0, 0]
    lines_all = width // LINE
    start_line = (origin // KY - ka * block_lines + block_lines + lines_all) % lines_all
    roll = (LINE - (origin % KY) * BANDS) % LINE
    scalars = jnp.stack([start_line, roll, core, pb]).astype(jnp.int32)

    chunks = [([window], [window_other])]
    for piece in arrived:
        one = permute(piece, lambda p, zz, c: (p ^ (1 + c), zz, c))
        two = permute(piece, lambda p, zz, c: (p ^ (2 - c), zz, c))
        three = permute(one, lambda p, zz, c: (p ^ (2 - c), zz, c))
        mine = [piece, one, two, three]
        chunks.append((mine, [sibling(m) for m in mine]))
    owns, shifts = [], []
    for mine, other in chunks:
        own, shift = prepare(scalars, mine, other, block, lines)
        owns.append(own)
        shifts.append(shift)

    index = jnp.arange(256, dtype=jnp.int32) // BANDS
    mask = (index[:, None] == index[None, :]).astype(BF16)
    factor = 1.0 / math.sqrt(float(width))
    out_scalars = jnp.stack([core, z * (2 * rows)]).astype(jnp.int32)
    branches = coupling.shape[1]
    results = []
    for group in range(GROUPS):
        lo, hi = group * branches // GROUPS, (group + 1) * branches // GROUPS
        mine, *sends = products(out_scalars, x[lo:hi], mask, owns, shifts, rows, factor)
        same, cross = mine, 0.0
        for number, piece in enumerate(sends, 1):
            e, flip = number // 2, number % 2
            got = permute(piece, lambda p, zz, c: (p, zz + e, c ^ flip)).astype(F32)
            if flip:
                cross = cross + got
            else:
                same = same + got
        results.append(
            jnp.where(core == 0, jnp.stack([same, cross]), jnp.stack([cross, same]))
        )
    return jnp.concatenate(results, axis=1)


def solution(mesh):
    return jax.shard_map(
        shards,
        mesh=mesh,
        in_specs=(P("ka", None), P("pb", None, None, "ka"), P("pb", "ka")),
        out_specs=P("pb", None, "ka", None),
        check_vma=False,
    )
```

```python
import functools
import math

import jax
import jax.numpy as jnp
from jax import lax
from jax.experimental import pallas as pl
from jax.experimental.pallas import tpu as pltpu
from jax.sharding import PartitionSpec as P

KY = 96
BANDS = 16
LINE = KY * BANDS
GROUPS = 3
F32 = jnp.float32
BF16 = jnp.bfloat16


def contract(a, b, dim_a, dim_b):
    return lax.dot_general(a, b, (((dim_a,), (dim_b,)), ((), ())), preferred_element_type=F32)


def cut_kernel(block, scalars, env_ref, coupling_ref, *refs):
    pieces, (window, give, sems) = refs[:-3], refs[-3:]
    n_z = len(pieces) + 1
    core, pb, z = scalars[2], scalars[3], scalars[4]

    def lanes(index):
        return pl.ds(pl.multiple_of(lax.rem(index + 2 * n_z, 2 * n_z) * block, 128), block)

    jobs = []
    for e in range(1, n_z):
        to = lax.rem(z - e + n_z, n_z)
        jobs.append((env_ref.at[:, lanes(2 * to - 1 + pb)], pieces[e - 1]))
    for w in range(4):
        jobs.append((env_ref.at[:, lanes(2 * z - 1 + w)], window.at[:, w * block : (w + 1) * block]))
    jobs.append((coupling_ref.at[1 - core], give))
    copies = [pltpu.make_async_copy(src, dst, sems.at[i]) for i, (src, dst) in enumerate(jobs)]
    for copy in copies:
        copy.start()
    for copy in copies:
        copy.wait()


def cut(scalars, envelopes, coupling, n_z, block):
    rows = envelopes.shape[0]
    shape = functools.partial(jax.ShapeDtypeStruct, dtype=BF16)
    outs = [shape((rows, block))] * (n_z - 1) + [shape((rows, 4 * block)), shape(coupling.shape[1:])]
    *pieces, window, give = pl.pallas_call(
        functools.partial(cut_kernel, block),
        in_specs=[pl.BlockSpec(memory_space=pltpu.SMEM)] + [pl.BlockSpec(memory_space=pl.ANY)] * 2,
        out_specs=[pl.BlockSpec(memory_space=pl.ANY)] * len(outs),
        out_shape=outs,
        scratch_shapes=[pltpu.SemaphoreType.DMA((n_z + 4,))],
        name="cut",
    )(scalars, envelopes, coupling)
    return pieces, window, give


def prep_kernel(pieces, block, lines, scalars, *refs):
    ins, (keep_ref, give_ref, window, sems) = refs[:pieces], refs[pieces:]
    core, pb = scalars[2], scalars[3]
    copies = []
    for index, src in enumerate(ins):
        offset = 0
        if pieces > 1:
            rel = (0, 1 + core, 2 - core, 3)[index]
            offset = pl.multiple_of((pb ^ rel) * block, 128)
        copy = pltpu.make_async_copy(src, window.at[:, pl.ds(offset, src.shape[1])], sems.at[index])
        copy.start()
        copies.append(copy)
    for copy in copies:
        copy.wait()
    for line in range(lines):
        to = slice(line * LINE, (line + 1) * LINE)
        own = window[:, (lines // 2 + line) * LINE : (lines // 2 + line + 1) * LINE]
        for out_ref, q in ((keep_ref, core), (give_ref, 1 - core)):
            out_ref[0, :, to] = own
            start_line, roll = scalars[5 + 2 * q], scalars[6 + 2 * q]
            lane = pl.multiple_of((start_line + line) * LINE, 128)
            shifted = window[:, pl.ds(lane, LINE)].astype(F32)
            out_ref[1, :, to] = pltpu.roll(shifted, roll, 1).astype(BF16)


def prepare(scalars, ins, block, lines):
    rows = ins[0].shape[0]
    pieces = len(ins)
    out = jax.ShapeDtypeStruct((2, rows, lines * LINE), BF16)
    return pl.pallas_call(
        functools.partial(prep_kernel, pieces, block, lines),
        in_specs=[pl.BlockSpec(memory_space=pltpu.SMEM)] + [pl.BlockSpec(memory_space=pl.ANY)] * pieces,
        out_specs=[pl.BlockSpec(memory_space=pltpu.VMEM)] * 2,
        out_shape=[out, out],
        scratch_shapes=[
            pltpu.VMEM((rows, 2 * lines * LINE), BF16),
            pltpu.SemaphoreType.DMA((pieces,)),
        ],
        compiler_params=pltpu.CompilerParams(vmem_limit_bytes=24 << 20),
        name="prepare",
    )(scalars, *ins)


def main_kernel(first, branches, factor, scalars, x_ref, mask_ref, *refs):
    sources = len(refs) // 2
    amps, (mine_ref, *sends, total) = refs[:sources], refs[sources:]
    step = pl.program_id(0)

    @pl.when(step == 0)
    def _():
        total[...] = jnp.zeros_like(total)

    for branch in range(branches):
        parts = []
        for tile in range(LINE // 256):
            lanes = slice(tile * 256, (tile + 1) * 256)
            matrix = jnp.concatenate([x_ref[first + branch, :, lanes]] * 16, axis=0) * mask_ref[...]
            own = jnp.concatenate([ref[0, :, lanes] for ref in amps], axis=0)
            parts.append(contract(own, matrix, 1, 0).astype(BF16))
        diff = jnp.concatenate(parts, axis=1)
        shifted = jnp.concatenate([ref[1] for ref in amps], axis=0)
        total[branch] += contract(shifted, diff, 1, 1)

    @pl.when(step == pl.num_programs(0) - 1)
    def _():
        core, z = scalars[2], scalars[4]
        rows = mine_ref.shape[1]
        states = total.shape[2]
        low = lax.broadcasted_iota(jnp.int32, (rows, states), 1) // rows % 2 == 0
        for branch in range(branches):
            for source in range(sources):
                piece = pltpu.roll(total[branch, source * rows : (source + 1) * rows] * factor, z * (2 * rows), 1)
                swapped = jnp.where(low, pltpu.roll(piece, states - rows, 1), pltpu.roll(piece, rows, 1))
                piece = jnp.where(core == 0, piece, swapped)
                if source == 0:
                    mine_ref[branch] = piece
                else:
                    sends[source - 1][branch] = piece.astype(BF16)


def products(scalars, x, mask, amps, first, branches, factor):
    sources, rows = len(amps), amps[0].shape[1]
    states = sources * rows
    lines = x.shape[2] // LINE
    piece = pl.BlockSpec((branches, rows, states), lambda i: (0, 0, 0))
    return pl.pallas_call(
        functools.partial(main_kernel, first, branches, factor),
        grid=(lines,),
        in_specs=[
            pl.BlockSpec(memory_space=pltpu.SMEM),
            pl.BlockSpec((x.shape[0], BANDS, LINE), lambda i: (0, 0, i)),
            pl.BlockSpec((256, 256), lambda i: (0, 0)),
        ]
        + [pl.BlockSpec((2, rows, LINE), lambda i: (0, 0, i))] * sources,
        out_specs=[piece] * sources,
        out_shape=[jax.ShapeDtypeStruct((branches, rows, states), F32 if i == 0 else BF16) for i in range(sources)],
        scratch_shapes=[pltpu.VMEM((branches, states, states), F32)],
        compiler_params=pltpu.CompilerParams(vmem_limit_bytes=40 << 20),
        cost_estimate=pl.CostEstimate(
            flops=4 * branches * states * states * lines * LINE,
            bytes_accessed=4 * states * lines * LINE,
            transcendentals=0,
        ),
        name="products",
    )(scalars, x, mask, *amps)


def band_kernel(scalars, coupling_ref, other_ref, x_ref):
    branches, _, count = other_ref.shape
    half = BANDS // 4
    size = min(count, 128)

    def iota(shape, dim):
        return lax.broadcasted_iota(jnp.int32, shape, dim)

    shape = (8 * BANDS, 32)
    row, col = iota(shape, 0), iota(shape, 1)
    term, v, c = row // BANDS, row % BANDS // half, row % half
    choice = jnp.where(term < 4, 4 * term + c, 16 + 4 * v + (term - 4))
    pick = (choice == col).astype(F32).astype(BF16)
    spread = []
    for by_a in (False, True):
        shape = (4 * size, size * BANDS)
        row, lane = iota(shape, 0), iota(shape, 1)
        band = lane % BANDS
        index = band // half if by_a else band % half
        hit = (row % size == lane // BANDS) & (row // size == index)
        spread.append(hit.astype(F32).astype(BF16))
    shape = (branches * BANDS, size * BANDS)
    row, lane = iota(shape, 0) % BANDS, iota(shape, 1) % BANDS
    keep_cond = (row // half == lane // half).astype(F32)
    keep_val = (row % half == lane % half).astype(F32)
    core = scalars[2]
    for mine in (True, False):
        tables = [coupling_ref[core, branch] if mine else other_ref[branch] for branch in range(branches)]
        terms = [contract(pick, table, 1, 0).astype(BF16) for table in tables]
        base = (core if mine else 1 - core) * (count * BANDS)
        for start in range(0, count, size):
            width = min(size, count - start)
            lanes = width * BANDS
            values = []
            for kind in range(2):
                rows = []
                for term in terms:
                    slabs = []
                    for index in range(4):
                        at = (4 * kind + index) * BANDS
                        slab = term[at : at + BANDS, start : start + width]
                        if width < size:
                            slab = jnp.concatenate([slab, jnp.zeros((BANDS, size - width), BF16)], axis=1)
                        slabs.append(slab)
                    rows.append(jnp.concatenate(slabs, axis=1))
                values.append(contract(jnp.concatenate(rows, axis=0), spread[kind][:, :lanes], 1, 0))
            total = (values[0] * keep_cond[:, :lanes] - values[1] * keep_val[:, :lanes]).astype(BF16)
            at = pl.multiple_of(base + start * BANDS, 128)
            for branch in range(branches):
                x_ref[branch, :, pl.ds(at, lanes)] = total[branch * BANDS : (branch + 1) * BANDS]


def band_matrices(scalars, coupling, other):
    branches, _, count = other.shape
    return pl.pallas_call(
        band_kernel,
        in_specs=[pl.BlockSpec(memory_space=pltpu.SMEM)] + [pl.BlockSpec(memory_space=pltpu.VMEM)] * 2,
        out_specs=pl.BlockSpec(memory_space=pltpu.VMEM),
        out_shape=jax.ShapeDtypeStruct((branches, BANDS, 2 * count * BANDS), BF16),
        compiler_params=pltpu.CompilerParams(vmem_limit_bytes=40 << 20),
        cost_estimate=pl.CostEstimate(flops=10**10, bytes_accessed=10**6, transcendentals=0),
        name="band_matrices",
    )(scalars, coupling, other)


def shards(envelopes, coupling, kq_map):
    n_pb, n_ka = lax.axis_size("pb"), lax.axis_size("ka")
    assert n_pb == 4 and n_ka % 2 == 0 and coupling.shape[0] == 2
    n_z = n_ka // 2
    rows, width = envelopes.shape
    block = width // n_ka
    block_lines = block // LINE
    lines = 2 * block_lines
    pb, ka = lax.axis_index("pb"), lax.axis_index("ka")
    z, core = ka // 2, ka % 2

    def permute(x, to):
        pairs = []
        for p in range(n_pb):
            for k in range(n_ka):
                tp, tz, tc = to(p, k // 2, k % 2)
                pairs.append((p * n_ka + k, tp * n_ka + (tz % n_z) * 2 + tc))
        return lax.ppermute(x, ("pb", "ka"), pairs)

    def sibling(x):
        return permute(x, lambda p, zz, c: (p, zz, 1 - c))

    origin = kq_map[:, 0]
    lines_all = width // LINE
    start_line = (origin // KY - ka * block_lines + block_lines + lines_all) % lines_all
    roll = (LINE - (origin % KY) * BANDS) % LINE
    turns = jnp.stack([start_line, roll], axis=1).reshape(-1)
    scalars = jnp.concatenate([jnp.stack([ka, ka, core, pb, z]), turns]).astype(jnp.int32)

    pieces, window, give = cut(scalars, envelopes, coupling, n_z, block)
    arrived = []
    for e in range(1, n_z):
        arrived.append(permute(pieces[e - 1], lambda p, zz, c: (p, zz - e, c)))
    x = band_matrices(scalars, coupling, sibling(give))

    amps = []
    keep, pass_on = prepare(scalars, [window], block, lines)
    amps += [keep, sibling(pass_on)]
    for piece in arrived:
        one = permute(piece, lambda p, zz, c: (p ^ (1 + c), zz, c))
        two = permute(piece, lambda p, zz, c: (p ^ (2 - c), zz, c))
        three = permute(one, lambda p, zz, c: (p ^ (2 - c), zz, c))
        keep, pass_on = prepare(scalars, [piece, one, two, three], block, lines)
        amps += [keep, sibling(pass_on)]

    index = jnp.arange(256, dtype=jnp.int32) // BANDS
    mask = (index[:, None] == index[None, :]).astype(BF16)
    factor = 1.0 / math.sqrt(float(width))
    branches = coupling.shape[1]
    results = []
    for group in range(GROUPS):
        lo, hi = group * branches // GROUPS, (group + 1) * branches // GROUPS
        mine, *sends = products(scalars, x, mask, amps, lo, hi - lo, factor)
        same, cross = mine, 0.0
        for number, piece in enumerate(sends, 1):
            e, flip = number // 2, number % 2
            got = permute(piece, lambda p, zz, c: (p, zz + e, c ^ flip)).astype(F32)
            if flip:
                cross = cross + got
            else:
                same = same + got
        results.append(
            jnp.where(core == 0, jnp.stack([same, cross]), jnp.stack([cross, same]))
        )
    return jnp.concatenate(results, axis=1)


def solution(mesh):
    return jax.shard_map(
        shards,
        mesh=mesh,
        in_specs=(P("ka", None), P("pb", None, None, "ka"), P("pb", "ka")),
        out_specs=P("pb", None, "ka", None),
        check_vma=False,
    )
```

```python
import functools
import math

import jax
import jax.numpy as jnp
from jax import lax
from jax.experimental import pallas as pl
from jax.experimental.pallas import tpu as pltpu
from jax.sharding import PartitionSpec as P

KY = 96
BANDS = 16
LINE = KY * BANDS
GROUPS = (5, 8)
F32 = jnp.float32
BF16 = jnp.bfloat16


def contract(a, b, dim_a, dim_b):
    return lax.dot_general(a, b, (((dim_a,), (dim_b,)), ((), ())), preferred_element_type=F32)


def place():
    ka = lax.axis_index("ka")
    return lax.axis_index("pb"), ka // 2, ka % 2


def cut_kernel(block, env_ref, coupling_ref, *refs):
    pieces, (window, give, sems) = refs[:-3], refs[-3:]
    n_z = len(pieces) + 1
    pb, z, core = place()

    def lanes(index):
        return pl.ds(pl.multiple_of(lax.rem(index + 2 * n_z, 2 * n_z) * block, 128), block)

    jobs = []
    for e in range(1, n_z):
        to = lax.rem(z - e + n_z, n_z)
        jobs.append((env_ref.at[:, lanes(2 * to - 1 + pb)], pieces[e - 1]))
    for w in range(4):
        jobs.append((env_ref.at[:, lanes(2 * z - 1 + w)], window.at[:, w * block : (w + 1) * block]))
    jobs.append((coupling_ref.at[1 - core], give))
    copies = [pltpu.make_async_copy(src, dst, sems.at[i]) for i, (src, dst) in enumerate(jobs)]
    for copy in copies:
        copy.start()
    for copy in copies:
        copy.wait()


def cut(envelopes, coupling, n_z, block):
    rows = envelopes.shape[0]
    shape = functools.partial(jax.ShapeDtypeStruct, dtype=BF16)
    outs = [shape((rows, block))] * (n_z - 1) + [shape((rows, 4 * block)), shape(coupling.shape[1:])]
    *pieces, window, give = pl.pallas_call(
        functools.partial(cut_kernel, block),
        in_specs=[pl.BlockSpec(memory_space=pl.ANY)] * 2,
        out_specs=[pl.BlockSpec(memory_space=pltpu.VMEM)] * len(outs),
        out_shape=outs,
        scratch_shapes=[pltpu.SemaphoreType.DMA((n_z + 4,))],
        name="cut",
    )(envelopes, coupling)
    return pieces, window, give


def prep_kernel(block, lines, lines_all, kq_ref, *refs):
    ins, (keep_ref, give_ref, window, sems) = refs[:-4], refs[-4:]
    pb, z, core = place()
    copies = []
    for index, src in enumerate(ins):
        offset = 0
        if len(ins) > 1:
            rel = (0, 1 + core, 2 - core, 3)[index]
            offset = pl.multiple_of((pb ^ rel) * block, 128)
        copy = pltpu.make_async_copy(src, window.at[:, pl.ds(offset, src.shape[1])], sems.at[index])
        copy.start()
        copies.append(copy)
    for copy in copies:
        copy.wait()
    half = lines // 2
    turns = []
    for q in (core, 1 - core):
        origin = kq_ref[q, 0]
        start_line = lax.rem(origin // KY - (2 * z + core) * half + half + lines_all, lines_all)
        turns.append((start_line, lax.rem(LINE - lax.rem(origin, KY) * BANDS, LINE)))
    for line in range(lines):
        to = slice(line * LINE, (line + 1) * LINE)
        own = window[:, (half + line) * LINE : (half + line + 1) * LINE]
        for out_ref, (start_line, turn) in zip((keep_ref, give_ref), turns):
            out_ref[0, :, to] = own
            lane = pl.multiple_of((start_line + line) * LINE, 128)
            shifted = window[:, pl.ds(lane, LINE)].astype(F32)
            out_ref[1, :, to] = pltpu.roll(shifted, turn, 1).astype(BF16)


def prepare(kq_map, ins, block, lines, lines_all):
    rows = ins[0].shape[0]
    out = jax.ShapeDtypeStruct((2, rows, lines * LINE), BF16)
    return pl.pallas_call(
        functools.partial(prep_kernel, block, lines, lines_all),
        in_specs=[pl.BlockSpec(memory_space=pltpu.SMEM)] + [pl.BlockSpec(memory_space=pl.ANY)] * len(ins),
        out_specs=[pl.BlockSpec(memory_space=pltpu.VMEM)] * 2,
        out_shape=[out, out],
        scratch_shapes=[
            pltpu.VMEM((rows, 2 * lines * LINE), BF16),
            pltpu.SemaphoreType.DMA((len(ins),)),
        ],
        compiler_params=pltpu.CompilerParams(vmem_limit_bytes=24 << 20),
        name="prepare",
    )(kq_map, *ins)


def main_kernel(sources, first, branches, factor, x_ref, mask_ref, *refs):
    amps, (mine_ref, *sends, total) = refs[:sources], refs[sources:]
    step = pl.program_id(0)

    @pl.when(step == 0)
    def _():
        total[...] = jnp.zeros_like(total)

    for branch in range(branches):
        parts = []
        for tile in range(LINE // 256):
            lanes = slice(tile * 256, (tile + 1) * 256)
            matrix = jnp.concatenate([x_ref[first + branch, :, lanes]] * 16, axis=0) * mask_ref[...]
            own = jnp.concatenate([ref[0, :, lanes] for ref in amps], axis=0)
            parts.append(contract(own, matrix, 1, 0).astype(BF16))
        diff = jnp.concatenate(parts, axis=1)
        shifted = jnp.concatenate([ref[1] for ref in amps], axis=0)
        total[branch] += contract(shifted, diff, 1, 1)

    @pl.when(step == pl.num_programs(0) - 1)
    def _():
        _, z, core = place()
        states = total.shape[2]
        rows = states // sources
        col = lax.broadcasted_iota(jnp.int32, (states, states), 0)
        target = lax.broadcasted_iota(jnp.int32, (states, states), 1)
        source = lax.rem(col // rows + 2 * z, sources)
        home = (source // 2 * 2 + (source % 2 ^ core)) * rows + col % rows
        to_home = (home == target).astype(F32).astype(BF16)
        for branch in range(branches):
            value = total[branch] * factor
            high = value.astype(BF16)
            moved = contract(high, to_home, 1, 0)
            rest = value[: 2 * rows] - high[: 2 * rows].astype(F32)
            middle = rest.astype(BF16)
            low = (rest - middle.astype(F32)).astype(BF16)
            mine_ref[branch] = moved[: 2 * rows] + contract(middle, to_home, 1, 0) + contract(low, to_home, 1, 0)
            for chip, send in enumerate(sends, 1):
                send[branch] = moved[chip * 2 * rows : (chip + 1) * 2 * rows].astype(BF16)


def products(x, mask, amps, first, branches, factor):
    sources, rows = len(amps), amps[0].shape[1]
    states = sources * rows
    lines = x.shape[2] // LINE
    piece = pl.BlockSpec((branches, 2 * rows, states), lambda i: (0, 0, 0))
    shape = (branches, 2 * rows, states)
    return pl.pallas_call(
        functools.partial(main_kernel, sources, first, branches, factor),
        grid=(lines,),
        in_specs=[
            pl.BlockSpec((x.shape[0], BANDS, LINE), lambda i: (0, 0, i)),
            pl.BlockSpec((256, 256), lambda i: (0, 0)),
        ]
        + [pl.BlockSpec((2, rows, LINE), lambda i: (0, 0, i))] * sources,
        out_specs=[piece] * (sources // 2),
        out_shape=[jax.ShapeDtypeStruct(shape, F32 if i == 0 else BF16) for i in range(sources // 2)],
        scratch_shapes=[pltpu.VMEM((branches, states, states), F32)],
        compiler_params=pltpu.CompilerParams(vmem_limit_bytes=40 << 20),
        cost_estimate=pl.CostEstimate(
            flops=4 * branches * states * states * lines * LINE,
            bytes_accessed=4 * states * lines * LINE,
            transcendentals=0,
        ),
        name="products",
    )(x, mask, *amps)


def band_kernel(coupling_ref, other_ref, x_ref):
    branches, _, count = other_ref.shape
    half = BANDS // 4
    size = min(count, 128)

    def iota(shape, dim):
        return lax.broadcasted_iota(jnp.int32, shape, dim)

    shape = (8 * BANDS, 32)
    row, col = iota(shape, 0), iota(shape, 1)
    term, v, c = row // BANDS, row % BANDS // half, row % half
    choice = jnp.where(term < 4, 4 * term + c, 16 + 4 * v + (term - 4))
    pick = (choice == col).astype(F32).astype(BF16)
    spread = []
    for by_a in (False, True):
        shape = (4 * size, size * BANDS)
        row, lane = iota(shape, 0), iota(shape, 1)
        band = lane % BANDS
        index = band // half if by_a else band % half
        hit = (row % size == lane // BANDS) & (row // size == index)
        spread.append(hit.astype(F32).astype(BF16))
    shape = (branches * BANDS, size * BANDS)
    row, lane = iota(shape, 0) % BANDS, iota(shape, 1) % BANDS
    keep_cond = (row // half == lane // half).astype(F32)
    keep_val = (row % half == lane % half).astype(F32)
    _, _, core = place()
    for mine in (True, False):
        tables = [coupling_ref[core, branch] if mine else other_ref[branch] for branch in range(branches)]
        terms = [contract(pick, table, 1, 0).astype(BF16) for table in tables]
        base = (core if mine else 1 - core) * (count * BANDS)
        for start in range(0, count, size):
            width = min(size, count - start)
            lanes = width * BANDS
            values = []
            for kind in range(2):
                rows = []
                for term in terms:
                    slabs = []
                    for index in range(4):
                        at = (4 * kind + index) * BANDS
                        slab = term[at : at + BANDS, start : start + width]
                        if width < size:
                            slab = jnp.concatenate([slab, jnp.zeros((BANDS, size - width), BF16)], axis=1)
                        slabs.append(slab)
                    rows.append(jnp.concatenate(slabs, axis=1))
                values.append(contract(jnp.concatenate(rows, axis=0), spread[kind][:, :lanes], 1, 0))
            total = (values[0] * keep_cond[:, :lanes] - values[1] * keep_val[:, :lanes]).astype(BF16)
            at = pl.multiple_of(base + start * BANDS, 128)
            for branch in range(branches):
                x_ref[branch, :, pl.ds(at, lanes)] = total[branch * BANDS : (branch + 1) * BANDS]


def band_matrices(coupling, other):
    branches, _, count = other.shape
    return pl.pallas_call(
        band_kernel,
        in_specs=[pl.BlockSpec(memory_space=pltpu.VMEM)] * 2,
        out_specs=pl.BlockSpec(memory_space=pltpu.VMEM),
        out_shape=jax.ShapeDtypeStruct((branches, BANDS, 2 * count * BANDS), BF16),
        compiler_params=pltpu.CompilerParams(vmem_limit_bytes=40 << 20),
        cost_estimate=pl.CostEstimate(flops=10**10, bytes_accessed=10**6, transcendentals=0),
        name="band_matrices",
    )(coupling, other)


def shards(envelopes, coupling, kq_map):
    n_pb, n_ka = lax.axis_size("pb"), lax.axis_size("ka")
    assert n_pb == 4 and n_ka % 2 == 0 and coupling.shape[0] == 2
    n_z = n_ka // 2
    rows, width = envelopes.shape
    block = width // n_ka
    lines, lines_all = 2 * block // LINE, width // LINE
    branches = coupling.shape[1]
    core = lax.axis_index("ka") % 2

    def permute(x, to):
        pairs = []
        for p in range(n_pb):
            for k in range(n_ka):
                tp, tz, tc = to(p, k // 2, k % 2)
                pairs.append((p * n_ka + k, tp * n_ka + (tz % n_z) * 2 + tc))
        return lax.ppermute(x, ("pb", "ka"), pairs)

    def sibling(x):
        return permute(x, lambda p, zz, c: (p, zz, 1 - c))

    pieces, window, give = cut(envelopes, coupling, n_z, block)
    arrived = []
    for e in range(1, n_z):
        arrived.append(permute(pieces[e - 1], lambda p, zz, c: (p, zz - e, c)))
    keep, pass_on = prepare(kq_map, [window], block, lines, lines_all)
    amps = [keep, sibling(pass_on)]
    x = band_matrices(coupling, sibling(give))
    arrived[0], x, amps[0] = lax.optimization_barrier((arrived[0], x, amps[0]))

    for piece in arrived:
        one = permute(piece, lambda p, zz, c: (p ^ (1 + c), zz, c))
        two = permute(piece, lambda p, zz, c: (p ^ (2 - c), zz, c))
        three = permute(one, lambda p, zz, c: (p ^ (2 - c), zz, c))
        keep, pass_on = prepare(kq_map, [piece, one, two, three], block, lines, lines_all)
        amps += [keep, sibling(pass_on)]

    index = jnp.arange(256, dtype=jnp.int32) // BANDS
    mask = (index[:, None] == index[None, :]).astype(BF16)
    factor = 1.0 / math.sqrt(float(width))
    edges = [0] + [edge * branches // 9 for edge in GROUPS] + [branches]
    received, mine, other = [], [], []
    for lo, hi in zip(edges[:-1], edges[1:]):
        if len(received) >= 2:
            received[-2], x = lax.optimization_barrier((received[-2], x))
        own, *sends = products(x, mask, amps, lo, hi - lo, factor)
        received.append([own] + [permute(p, lambda p, zz, c: (p, zz + e, c)) for e, p in enumerate(sends, 1)])
    for parts in received:
        total = parts[0]
        for part in parts[1:]:
            total = total + part.astype(F32)
        mine.append(total[:, :rows])
        other.append(sibling(total[:, rows:]))
    mine, other = jnp.concatenate(mine, axis=0), jnp.concatenate(other, axis=0)
    return jnp.where(core == 0, jnp.stack([mine, other]), jnp.stack([other, mine]))


def solution(mesh):
    return jax.shard_map(
        shards,
        mesh=mesh,
        in_specs=(P("ka", None), P("pb", None, None, "ka"), P("pb", "ka")),
        out_specs=P("pb", None, "ka", None),
        check_vma=False,
    )
```

```python
import functools
import math

import jax
import jax.numpy as jnp
from jax import lax
from jax.experimental import pallas as pl
from jax.experimental.pallas import tpu as pltpu
from jax.sharding import PartitionSpec as P

KY = 96
BANDS = 16
LINE = KY * BANDS
GROUPS = (5, 8)
VMEM_ALL = 56 << 20
F32 = jnp.float32
BF16 = jnp.bfloat16


def contract(a, b, dim_a, dim_b):
    return lax.dot_general(a, b, (((dim_a,), (dim_b,)), ((), ())), preferred_element_type=F32)


def place():
    ka = lax.axis_index("ka")
    return lax.axis_index("pb"), ka // 2, ka % 2


def turns_of(kq_ref, q, block_lines, lines_all):
    _, z, core = place()
    origin = kq_ref[q, 0]
    step = lax.rem(origin // KY - (2 * z + core) * block_lines + block_lines + lines_all, lines_all) - block_lines
    base = jnp.where(step < 0, block_lines, 0)
    return base, base + step, lax.rem(LINE - lax.rem(origin, KY) * BANDS, LINE)


def cut_kernel(block, env_ref, coupling_ref, *refs):
    pieces, (window, give, sems) = refs[:-3], refs[-3:]
    n_z = len(pieces) + 1
    pb, z, core = place()
    part = block // 4

    def lanes(chip, index):
        return pl.ds(pl.multiple_of(lax.rem(8 * chip + index, 8 * n_z) * part, 128), part)

    jobs = []
    for e in range(1, n_z):
        to = lax.rem(z - e + n_z, n_z)
        for i in range(3):
            jobs.append((env_ref.at[:, lanes(to, 3 * pb + i)], pieces[e - 1].at[:, i * part : (i + 1) * part]))
    for i in range(12):
        jobs.append((env_ref.at[:, lanes(z, i)], window.at[:, i * part : (i + 1) * part]))
    jobs.append((coupling_ref.at[1 - core], give))
    copies = [pltpu.make_async_copy(src, dst, sems.at[i]) for i, (src, dst) in enumerate(jobs)]
    for copy in copies:
        copy.start()
    for copy in copies:
        copy.wait()


def cut(envelopes, coupling, n_z, block):
    rows = envelopes.shape[0]
    shape = functools.partial(jax.ShapeDtypeStruct, dtype=BF16)
    outs = [shape((rows, 3 * block // 4))] * (n_z - 1) + [shape((rows, 3 * block)), shape(coupling.shape[1:])]
    *pieces, window, give = pl.pallas_call(
        functools.partial(cut_kernel, block),
        in_specs=[pl.BlockSpec(memory_space=pl.ANY)] * 2,
        out_specs=[pl.BlockSpec(memory_space=pltpu.VMEM)] * len(outs),
        out_shape=outs,
        scratch_shapes=[pltpu.SemaphoreType.DMA((3 * n_z + 10,))],
        name="cut",
    )(envelopes, coupling)
    return pieces, window, give


def prep_kernel(lines_all, kq_ref, *refs):
    ins, (keep_ref, give_ref, window, sems) = refs[:-4], refs[-4:]
    pb, _, core = place()
    line = pl.program_id(0)
    block_lines = pl.num_programs(0) // 2

    @pl.when(line == 0)
    def _():
        copies = []
        for index, src in enumerate(ins):
            offset, size = 0, src.shape[1]
            if len(ins) > 1:
                rel = (0, 1 + core, 2 - core, 3)[index]
                offset = pl.multiple_of((pb ^ rel) * size, 128)
            copy = pltpu.make_async_copy(src, window.at[:, pl.ds(offset, size)], sems.at[index])
            copy.start()
            copies.append(copy)
        for copy in copies:
            copy.wait()

    for out_ref, q in ((keep_ref, core), (give_ref, 1 - core)):
        base, image, turn = turns_of(kq_ref, q, block_lines, lines_all)
        out_ref[0] = window[:, pl.ds(pl.multiple_of((base + line) * LINE, 128), LINE)]
        shifted = window[:, pl.ds(pl.multiple_of((image + line) * LINE, 128), LINE)].astype(F32)
        out_ref[1] = pltpu.roll(shifted, turn, 1).astype(BF16)


def prepare(kq_map, ins, block, lines_all):
    rows, lines = ins[0].shape[0], 2 * block // LINE
    out = jax.ShapeDtypeStruct((2, rows, lines * LINE), BF16)
    return pl.pallas_call(
        functools.partial(prep_kernel, lines_all),
        grid=(lines,),
        in_specs=[pl.BlockSpec(memory_space=pltpu.SMEM)] + [pl.BlockSpec(memory_space=pl.ANY)] * len(ins),
        out_specs=[pl.BlockSpec((2, rows, LINE), lambda i: (0, 0, i))] * 2,
        out_shape=[out, out],
        scratch_shapes=[
            pltpu.VMEM((rows, 3 * block), BF16),
            pltpu.SemaphoreType.DMA((len(ins),)),
        ],
        compiler_params=pltpu.CompilerParams(vmem_limit_bytes=VMEM_ALL),
        name="prepare",
    )(kq_map, *ins)


def main_kernel(sources, first, branches, factor, x_ref, mask_ref, *refs):
    amps, (mine_ref, *sends, total) = refs[:sources], refs[sources:]
    step = pl.program_id(0)

    @pl.when(step == 0)
    def _():
        total[...] = jnp.zeros_like(total)

    for branch in range(branches):
        parts = []
        for tile in range(LINE // 256):
            lanes = slice(tile * 256, (tile + 1) * 256)
            matrix = jnp.concatenate([x_ref[first + branch, :, lanes]] * 16, axis=0) * mask_ref[...]
            own = jnp.concatenate([ref[0, :, lanes] for ref in amps], axis=0)
            parts.append(contract(own, matrix, 1, 0).astype(BF16))
        diff = jnp.concatenate(parts, axis=1)
        shifted = jnp.concatenate([ref[1] for ref in amps], axis=0)
        total[branch] += contract(shifted, diff, 1, 1)

    @pl.when(step == pl.num_programs(0) - 1)
    def _():
        _, z, core = place()
        states = total.shape[2]
        rows = states // sources
        col = lax.broadcasted_iota(jnp.int32, (states, states), 0)
        target = lax.broadcasted_iota(jnp.int32, (states, states), 1)
        source = lax.rem(col // rows + 2 * z, sources)
        home = (source // 2 * 2 + (source % 2 ^ core)) * rows + col % rows
        to_home = (home == target).astype(F32).astype(BF16)
        for branch in range(branches):
            value = total[branch] * factor
            high = value.astype(BF16)
            moved = contract(high, to_home, 1, 0)
            rest = value[: 2 * rows] - high[: 2 * rows].astype(F32)
            middle = rest.astype(BF16)
            low = (rest - middle.astype(F32)).astype(BF16)
            mine_ref[branch] = moved[: 2 * rows] + contract(middle, to_home, 1, 0) + contract(low, to_home, 1, 0)
            for chip, send in enumerate(sends, 1):
                send[branch] = moved[chip * 2 * rows : (chip + 1) * 2 * rows].astype(BF16)


def products(x, mask, amps, first, branches, factor):
    sources, rows = len(amps), amps[0].shape[1]
    states = sources * rows
    lines = x.shape[2] // LINE
    piece = pl.BlockSpec((branches, 2 * rows, states), lambda i: (0, 0, 0))
    shape = (branches, 2 * rows, states)
    return pl.pallas_call(
        functools.partial(main_kernel, sources, first, branches, factor),
        grid=(lines,),
        in_specs=[
            pl.BlockSpec((x.shape[0], BANDS, LINE), lambda i: (0, 0, i)),
            pl.BlockSpec((256, 256), lambda i: (0, 0)),
        ]
        + [pl.BlockSpec((2, rows, LINE), lambda i: (0, 0, i))] * sources,
        out_specs=[piece] * (sources // 2),
        out_shape=[jax.ShapeDtypeStruct(shape, F32 if i == 0 else BF16) for i in range(sources // 2)],
        scratch_shapes=[pltpu.VMEM((branches, states, states), F32)],
        compiler_params=pltpu.CompilerParams(vmem_limit_bytes=VMEM_ALL),
        cost_estimate=pl.CostEstimate(
            flops=4 * branches * states * states * lines * LINE,
            bytes_accessed=4 * states * lines * LINE,
            transcendentals=0,
        ),
        name="products",
    )(x, mask, *amps)


def band_kernel(block_lines, lines_all, kq_ref, coupling_ref, other_ref, next_ref, x_ref):
    branches, _, count = other_ref.shape
    half = BANDS // 4
    size = min(count, 128)

    def iota(shape, dim):
        return lax.broadcasted_iota(jnp.int32, shape, dim)

    shape = (8 * BANDS, 32)
    row, col = iota(shape, 0), iota(shape, 1)
    term, v, c = row // BANDS, row % BANDS // half, row % half
    choice = jnp.where(term < 4, 4 * term + c, 16 + 4 * v + (term - 4))
    pick = (choice == col).astype(F32).astype(BF16)
    spread = []
    for by_a in (False, True):
        shape = (4 * size, size * BANDS)
        row, lane = iota(shape, 0), iota(shape, 1)
        band = lane % BANDS
        index = band // half if by_a else band % half
        hit = (row % size == lane // BANDS) & (row // size == index)
        spread.append(hit.astype(F32).astype(BF16))
    shape = (branches * BANDS, size * BANDS)
    row, lane = iota(shape, 0) % BANDS, iota(shape, 1) % BANDS
    keep_cond = (row // half == lane // half).astype(F32)
    keep_val = (row % half == lane % half).astype(F32)
    _, _, core = place()
    base, _, _ = turns_of(kq_ref, core, block_lines, lines_all)
    late = jnp.where(base > 0, 1, 0)
    for part in range(2):
        block = part + late
        terms = []
        for branch in range(branches):
            table = jnp.where(block == core, coupling_ref[core, branch], other_ref[branch])
            table = jnp.where(block == 2, next_ref[branch], table)
            terms.append(contract(pick, table, 1, 0).astype(BF16))
        for start in range(0, count, size):
            width = min(size, count - start)
            lanes = width * BANDS
            values = []
            for kind in range(2):
                rows = []
                for term in terms:
                    slabs = []
                    for index in range(4):
                        at = (4 * kind + index) * BANDS
                        slab = term[at : at + BANDS, start : start + width]
                        if width < size:
                            slab = jnp.concatenate([slab, jnp.zeros((BANDS, size - width), BF16)], axis=1)
                        slabs.append(slab)
                    rows.append(jnp.concatenate(slabs, axis=1))
                values.append(contract(jnp.concatenate(rows, axis=0), spread[kind][:, :lanes], 1, 0))
            total = (values[0] * keep_cond[:, :lanes] - values[1] * keep_val[:, :lanes]).astype(BF16)
            at = (part * count + start) * BANDS
            for branch in range(branches):
                x_ref[branch, :, at : at + lanes] = total[branch * BANDS : (branch + 1) * BANDS]


def band_matrices(kq_map, coupling, other, following, lines_all):
    branches, _, count = other.shape
    return pl.pallas_call(
        functools.partial(band_kernel, count // KY, lines_all),
        in_specs=[pl.BlockSpec(memory_space=pltpu.SMEM)] + [pl.BlockSpec(memory_space=pltpu.VMEM)] * 3,
        out_specs=pl.BlockSpec(memory_space=pltpu.VMEM),
        out_shape=jax.ShapeDtypeStruct((branches, BANDS, 2 * count * BANDS), BF16),
        compiler_params=pltpu.CompilerParams(vmem_limit_bytes=40 << 20),
        cost_estimate=pl.CostEstimate(flops=10**10, bytes_accessed=10**6, transcendentals=0),
        name="band_matrices",
    )(kq_map, coupling, other, following)


def shards(envelopes, coupling, kq_map):
    n_pb, n_ka = lax.axis_size("pb"), lax.axis_size("ka")
    assert n_pb == 4 and n_ka % 2 == 0 and coupling.shape[0] == 2
    n_z = n_ka // 2
    rows, width = envelopes.shape
    block = width // n_ka
    lines_all = width // LINE
    branches = coupling.shape[1]
    core = lax.axis_index("ka") % 2

    def permute(x, to):
        pairs = []
        for p in range(n_pb):
            for k in range(n_ka):
                tp, tz, tc = to(p, k // 2, k % 2)
                pairs.append((p * n_ka + k, tp * n_ka + (tz % n_z) * 2 + tc))
        return lax.ppermute(x, ("pb", "ka"), pairs)

    def sibling(x):
        return permute(x, lambda p, zz, c: (p, zz, 1 - c))

    def passed_down(e):
        return lambda x: permute(x, lambda p, zz, c: (p, zz - e, c))

    pieces, window, give = cut(envelopes, coupling, n_z, block)
    near = sorted({1, n_z - 1})
    far = [e for e in range(2, n_z - 1)]
    arrived = {e: passed_down(e)(pieces[e - 1]) for e in near}
    other_table = sibling(give)
    first_table = jnp.where(core == 0, lax.dynamic_index_in_dim(coupling, core, 0, keepdims=False), other_table)
    next_table = passed_down(1)(first_table)
    keep, pass_on = prepare(kq_map, [window], block, lines_all)
    waiting = [pieces[e - 1] for e in far]
    keep, pass_on, *waiting = lax.optimization_barrier((keep, pass_on, *waiting))
    for e, piece in zip(far, waiting):
        arrived[e] = passed_down(e)(piece)
    amps = {0: (keep, sibling(pass_on))}
    x = band_matrices(kq_map, coupling, other_table, next_table, lines_all)
    arrived[1], x = lax.optimization_barrier((arrived[1], x))

    for e in near + far:
        piece = arrived[e]
        one = permute(piece, lambda p, zz, c: (p ^ (1 + c), zz, c))
        two = permute(piece, lambda p, zz, c: (p ^ (2 - c), zz, c))
        three = permute(one, lambda p, zz, c: (p ^ (2 - c), zz, c))
        keep, pass_on = prepare(kq_map, [piece, one, two, three], block, lines_all)
        amps[e] = (keep, sibling(pass_on))
    amps = [half for e in range(n_z) for half in amps[e]]

    index = jnp.arange(256, dtype=jnp.int32) // BANDS
    mask = (index[:, None] == index[None, :]).astype(BF16)
    factor = 1.0 / math.sqrt(float(width))
    edges = [0] + [edge * branches // 9 for edge in GROUPS] + [branches]
    received, mine, other = [], [], []
    for lo, hi in zip(edges[:-1], edges[1:]):
        if len(received) >= 2:
            received[-2], x = lax.optimization_barrier((received[-2], x))
        own, *sends = products(x, mask, amps, lo, hi - lo, factor)
        own, x = lax.optimization_barrier((own, x))
        received.append([own] + [permute(p, lambda p, zz, c: (p, zz + e, c)) for e, p in enumerate(sends, 1)])
    for parts in received:
        total = parts[0]
        for part in parts[1:]:
            total = total + part.astype(F32)
        mine.append(total[:, :rows])
        other.append(sibling(total[:, rows:]))
    mine, other = jnp.concatenate(mine, axis=0), jnp.concatenate(other, axis=0)
    return jnp.where(core == 0, jnp.stack([mine, other]), jnp.stack([other, mine]))


def solution(mesh):
    return jax.shard_map(
        shards,
        mesh=mesh,
        in_specs=(P("ka", None), P("pb", None, None, "ka"), P("pb", "ka")),
        out_specs=P("pb", None, "ka", None),
        check_vma=False,
    )
```

```python
import functools
import math

import jax
import jax.numpy as jnp
from jax import lax
from jax.experimental import pallas as pl
from jax.experimental.pallas import tpu as pltpu
from jax.sharding import PartitionSpec as P

KY = 96
BANDS = 16
LINE = KY * BANDS
GROUPS = (5, 8)
F32 = jnp.float32
BF16 = jnp.bfloat16


def contract(a, b, dim_a, dim_b):
    return lax.dot_general(a, b, (((dim_a,), (dim_b,)), ((), ())), preferred_element_type=F32)


def place():
    ka = lax.axis_index("ka")
    return lax.axis_index("pb"), ka // 2, ka % 2


def turns_of(kq_ref, q, block_lines, lines_all):
    _, z, core = place()
    origin = kq_ref[q, 0]
    step = lax.rem(origin // KY - (2 * z + core) * block_lines + block_lines + lines_all, lines_all) - block_lines
    base = jnp.where(step < 0, block_lines, 0)
    return base, base + step, lax.rem(LINE - lax.rem(origin, KY) * BANDS, LINE)


def cut_kernel(block, env_ref, coupling_ref, *refs):
    pieces, (window, give, sems) = refs[:-3], refs[-3:]
    n_z = len(pieces) + 1
    pb, z, core = place()
    part = block // 4

    def lanes(chip, index):
        return pl.ds(pl.multiple_of(lax.rem(8 * chip + index, 8 * n_z) * part, 128), part)

    jobs = []
    for e in range(1, n_z):
        to = lax.rem(z - e + n_z, n_z)
        for i in range(3):
            jobs.append((env_ref.at[:, lanes(to, 3 * pb + i)], pieces[e - 1].at[:, i * part : (i + 1) * part]))
    for i in range(12):
        jobs.append((env_ref.at[:, lanes(z, i)], window.at[:, i * part : (i + 1) * part]))
    jobs.append((coupling_ref.at[1 - core], give))
    copies = [pltpu.make_async_copy(src, dst, sems.at[i]) for i, (src, dst) in enumerate(jobs)]
    for copy in copies:
        copy.start()
    for copy in copies:
        copy.wait()


def cut(envelopes, coupling, n_z, block):
    rows = envelopes.shape[0]
    shape = functools.partial(jax.ShapeDtypeStruct, dtype=BF16)
    outs = [shape((rows, 3 * block // 4))] * (n_z - 1) + [shape((rows, 3 * block)), shape(coupling.shape[1:])]
    *pieces, window, give = pl.pallas_call(
        functools.partial(cut_kernel, block),
        in_specs=[pl.BlockSpec(memory_space=pl.ANY)] * 2,
        out_specs=[pl.BlockSpec(memory_space=pltpu.VMEM)] * len(outs),
        out_shape=outs,
        scratch_shapes=[pltpu.SemaphoreType.DMA((3 * n_z + 10,))],
        name="cut",
    )(envelopes, coupling)
    return pieces, window, give


def prep_kernel(block_lines, lines_all, for_other, kq_ref, *refs):
    ins, (out_ref, window) = refs[:-2], refs[-2:]
    pb, _, core = place()
    q = 1 - core if for_other else core
    base, image, turn = turns_of(kq_ref, q, block_lines, lines_all)
    if len(ins) == 1:
        window = ins[0]
    else:
        for rel, src in zip((0, 1 + core, 2 - core, 3), ins):
            size = src.shape[1]
            window[:, pl.ds(pl.multiple_of((pb ^ rel) * size, 128), size)] = src[...]
    for line in range(2 * block_lines):
        to = slice(line * LINE, (line + 1) * LINE)
        out_ref[0, :, to] = window[:, pl.ds(pl.multiple_of((base + line) * LINE, 128), LINE)]
        shifted = window[:, pl.ds(pl.multiple_of((image + line) * LINE, 128), LINE)].astype(F32)
        out_ref[1, :, to] = pltpu.roll(shifted, turn, 1).astype(BF16)


def prepare(kq_map, ins, block, lines_all, for_other):
    rows = ins[0].shape[0]
    return pl.pallas_call(
        functools.partial(prep_kernel, block // LINE, lines_all, for_other),
        in_specs=[pl.BlockSpec(memory_space=pltpu.SMEM)] + [pl.BlockSpec(memory_space=pltpu.VMEM)] * len(ins),
        out_specs=pl.BlockSpec(memory_space=pltpu.VMEM),
        out_shape=jax.ShapeDtypeStruct((2, rows, 2 * block), BF16),
        scratch_shapes=[pltpu.VMEM((rows, 3 * block), BF16)],
        compiler_params=pltpu.CompilerParams(vmem_limit_bytes=16 << 20),
        name="prepare_other" if for_other else "prepare_own",
    )(kq_map, *ins)


def main_kernel(sources, first, branches, factor, x_ref, *refs):
    amps, (mine_ref, *sends, total, mask) = refs[:sources], refs[sources:]
    shape = mask.shape
    same = lax.broadcasted_iota(jnp.int32, shape, 0) // BANDS == lax.broadcasted_iota(jnp.int32, shape, 1) // BANDS
    mask[...] = same.astype(F32).astype(BF16)
    for line in range(x_ref.shape[2] // LINE):
        to = slice(line * LINE, (line + 1) * LINE)
        for branch in range(branches):
            parts = []
            for tile in range(LINE // 256):
                lanes = slice(line * LINE + tile * 256, line * LINE + (tile + 1) * 256)
                matrix = jnp.concatenate([x_ref[first + branch, :, lanes]] * 16, axis=0) * mask[...]
                own = jnp.concatenate([ref[0, :, lanes] for ref in amps], axis=0)
                parts.append(contract(own, matrix, 1, 0).astype(BF16))
            shifted = jnp.concatenate([ref[1, :, to] for ref in amps], axis=0)
            part = contract(shifted, jnp.concatenate(parts, axis=1), 1, 1)
            total[branch] = part if line == 0 else total[branch] + part
    _, z, core = place()
    states = total.shape[2]
    rows = states // sources
    col = lax.broadcasted_iota(jnp.int32, (states, states), 0)
    target = lax.broadcasted_iota(jnp.int32, (states, states), 1)
    source = lax.rem(col // rows + 2 * z, sources)
    home = (source // 2 * 2 + (source % 2 ^ core)) * rows + col % rows
    to_home = (home == target).astype(F32).astype(BF16)
    for branch in range(branches):
        value = total[branch] * factor
        high = value.astype(BF16)
        moved = contract(high, to_home, 1, 0)
        rest = value[: 2 * rows] - high[: 2 * rows].astype(F32)
        middle = rest.astype(BF16)
        low = (rest - middle.astype(F32)).astype(BF16)
        mine_ref[branch] = moved[: 2 * rows] + contract(middle, to_home, 1, 0) + contract(low, to_home, 1, 0)
        for chip, send in enumerate(sends, 1):
            send[branch] = moved[chip * 2 * rows : (chip + 1) * 2 * rows].astype(BF16)


def products(x, amps, first, branches, factor):
    sources, rows = len(amps), amps[0].shape[1]
    states, width = sources * rows, x.shape[2]
    shape = (branches, 2 * rows, states)
    return pl.pallas_call(
        functools.partial(main_kernel, sources, first, branches, factor),
        in_specs=[pl.BlockSpec(memory_space=pltpu.VMEM)] * (1 + sources),
        out_specs=[pl.BlockSpec(memory_space=pltpu.VMEM)] * (sources // 2),
        out_shape=[jax.ShapeDtypeStruct(shape, F32 if i == 0 else BF16) for i in range(sources // 2)],
        scratch_shapes=[pltpu.VMEM((branches, states, states), F32), pltpu.VMEM((256, 256), BF16)],
        compiler_params=pltpu.CompilerParams(vmem_limit_bytes=32 << 20),
        cost_estimate=pl.CostEstimate(
            flops=4 * branches * states * states * width, bytes_accessed=4 * states * width, transcendentals=0
        ),
        name="products",
    )(x, *amps)


def band_kernel(block_lines, lines_all, kq_ref, coupling_ref, other_ref, next_ref, x_ref):
    branches, _, count = other_ref.shape
    half = BANDS // 4
    size = min(count, 128)

    def iota(shape, dim):
        return lax.broadcasted_iota(jnp.int32, shape, dim)

    shape = (8 * BANDS, 32)
    row, col = iota(shape, 0), iota(shape, 1)
    term, v, c = row // BANDS, row % BANDS // half, row % half
    choice = jnp.where(term < 4, 4 * term + c, 16 + 4 * v + (term - 4))
    pick = (choice == col).astype(F32).astype(BF16)
    spread = []
    for by_a in (False, True):
        shape = (4 * size, size * BANDS)
        row, lane = iota(shape, 0), iota(shape, 1)
        band = lane % BANDS
        index = band // half if by_a else band % half
        hit = (row % size == lane // BANDS) & (row // size == index)
        spread.append(hit.astype(F32).astype(BF16))
    shape = (branches * BANDS, size * BANDS)
    row, lane = iota(shape, 0) % BANDS, iota(shape, 1) % BANDS
    keep_cond = (row // half == lane // half).astype(F32)
    keep_val = (row % half == lane % half).astype(F32)
    _, _, core = place()
    base, _, _ = turns_of(kq_ref, core, block_lines, lines_all)
    late = jnp.where(base > 0, 1, 0)
    for part in range(2):
        block = part + late
        terms = []
        for branch in range(branches):
            table = jnp.where(block == core, coupling_ref[core, branch], other_ref[branch])
            table = jnp.where(block == 2, next_ref[branch], table)
            terms.append(contract(pick, table, 1, 0).astype(BF16))
        for start in range(0, count, size):
            width = min(size, count - start)
            lanes = width * BANDS
            values = []
            for kind in range(2):
                rows = []
                for term in terms:
                    slabs = []
                    for index in range(4):
                        at = (4 * kind + index) * BANDS
                        slab = term[at : at + BANDS, start : start + width]
                        if width < size:
                            slab = jnp.concatenate([slab, jnp.zeros((BANDS, size - width), BF16)], axis=1)
                        slabs.append(slab)
                    rows.append(jnp.concatenate(slabs, axis=1))
                values.append(contract(jnp.concatenate(rows, axis=0), spread[kind][:, :lanes], 1, 0))
            total = (values[0] * keep_cond[:, :lanes] - values[1] * keep_val[:, :lanes]).astype(BF16)
            at = (part * count + start) * BANDS
            for branch in range(branches):
                x_ref[branch, :, at : at + lanes] = total[branch * BANDS : (branch + 1) * BANDS]


def band_matrices(kq_map, coupling, other, following, lines_all):
    branches, _, count = other.shape
    return pl.pallas_call(
        functools.partial(band_kernel, count // KY, lines_all),
        in_specs=[pl.BlockSpec(memory_space=pltpu.SMEM)] + [pl.BlockSpec(memory_space=pltpu.VMEM)] * 3,
        out_specs=pl.BlockSpec(memory_space=pltpu.VMEM),
        out_shape=jax.ShapeDtypeStruct((branches, BANDS, 2 * count * BANDS), BF16),
        compiler_params=pltpu.CompilerParams(vmem_limit_bytes=40 << 20),
        cost_estimate=pl.CostEstimate(flops=10**10, bytes_accessed=10**6, transcendentals=0),
        name="band_matrices",
    )(kq_map, coupling, other, following)


def shards(envelopes, coupling, kq_map):
    n_pb, n_ka = lax.axis_size("pb"), lax.axis_size("ka")
    assert n_pb == 4 and n_ka % 2 == 0 and coupling.shape[0] == 2
    n_z = n_ka // 2
    rows, width = envelopes.shape
    block = width // n_ka
    lines_all = width // LINE
    branches = coupling.shape[1]
    core = lax.axis_index("ka") % 2

    def permute(x, to):
        pairs = []
        for p in range(n_pb):
            for k in range(n_ka):
                tp, tz, tc = to(p, k // 2, k % 2)
                pairs.append((p * n_ka + k, tp * n_ka + (tz % n_z) * 2 + tc))
        return lax.ppermute(x, ("pb", "ka"), pairs)

    def sibling(x):
        return permute(x, lambda p, zz, c: (p, zz, 1 - c))

    def passed_down(e):
        return lambda x: permute(x, lambda p, zz, c: (p, zz - e, c))

    def passed_down(x, e):
        return permute(x, lambda p, zz, c: (p, zz - e, c))

    def prepared(ins, for_other):
        return prepare(kq_map, ins, block, lines_all, for_other)

    def after(x, *others):
        return lax.optimization_barrier((x, *others))[0]

    pieces, window, give = cut(envelopes, coupling, n_z, block)
    near = sorted({1, n_z - 1})
    far = [e for e in range(2, n_z - 1)]
    arrived = {1: passed_down(pieces[0], 1)}
    pass_on = prepared([window], True)
    if len(near) > 1:
        arrived[n_z - 1] = passed_down(after(pieces[n_z - 2], pass_on), n_z - 1)
    keep = prepared([after(window, pass_on)], False)
    for e in far:
        arrived[e] = passed_down(after(pieces[e - 1], keep), e)
    amps = {0: (keep, sibling(pass_on))}
    other_table = sibling(give)
    first_table = jnp.where(core == 0, lax.dynamic_index_in_dim(coupling, core, 0, keepdims=False), other_table)
    next_table = passed_down(first_table, 1)
    x = band_matrices(kq_map, coupling, other_table, next_table, lines_all)
    arrived[1] = after(arrived[1], x)

    for e in near + far:
        piece = arrived[e]
        one = permute(piece, lambda p, zz, c: (p ^ (1 + c), zz, c))
        two = permute(piece, lambda p, zz, c: (p ^ (2 - c), zz, c))
        three = permute(one, lambda p, zz, c: (p ^ (2 - c), zz, c))
        pass_on = prepared([piece, one, two, three], True)
        keep = prepared([after(piece, pass_on), one, two, three], False)
        amps[e] = (keep, sibling(pass_on))
    amps = [half for e in range(n_z) for half in amps[e]]

    factor = 1.0 / math.sqrt(float(width))
    edges = [0] + [edge * branches // 9 for edge in GROUPS] + [branches]
    received, mine, other = [], [], []
    for lo, hi in zip(edges[:-1], edges[1:]):
        if len(received) >= 2:
            x, received[-2] = lax.optimization_barrier((x, received[-2]))
        own, *sends = products(x, amps, lo, hi - lo, factor)
        x, own = lax.optimization_barrier((x, own))
        if received:
            own, received[-1] = lax.optimization_barrier((own, received[-1]))
        received.append([own] + [permute(p, lambda p, zz, c: (p, zz + e, c)) for e, p in enumerate(sends, 1)])
    for parts in received:
        total = parts[0]
        for part in parts[1:]:
            total = total + part.astype(F32)
        mine.append(total[:, :rows])
        other.append(sibling(total[:, rows:]))
    mine, other = jnp.concatenate(mine, axis=0), jnp.concatenate(other, axis=0)
    return jnp.where(core == 0, jnp.stack([mine, other]), jnp.stack([other, mine]))


def solution(mesh):
    return jax.shard_map(
        shards,
        mesh=mesh,
        in_specs=(P("ka", None), P("pb", None, None, "ka"), P("pb", "ka")),
        out_specs=P("pb", None, "ka", None),
        check_vma=False,
    )
```

```python
import functools
import math

import jax
import jax.numpy as jnp
from jax import lax
from jax.experimental import pallas as pl
from jax.experimental.pallas import tpu as pltpu
from jax.sharding import PartitionSpec as P

KY = 96
BANDS = 16
LINE = KY * BANDS
GROUPS = (5, 8)
F32 = jnp.float32
BF16 = jnp.bfloat16


def contract(a, b, dim_a, dim_b):
    return lax.dot_general(a, b, (((dim_a,), (dim_b,)), ((), ())), preferred_element_type=F32)


def place():
    ka = lax.axis_index("ka")
    return lax.axis_index("pb"), ka // 2, ka % 2


def turns_of(kq_ref, q, block_lines, lines_all):
    _, z, core = place()
    origin = kq_ref[q, 0]
    step = lax.rem(origin // KY - (2 * z + core) * block_lines + block_lines + lines_all, lines_all) - block_lines
    base = jnp.where(step < 0, block_lines, 0)
    return base, base + step, lax.rem(LINE - lax.rem(origin, KY) * BANDS, LINE)


def cut_kernel(block, env_ref, coupling_ref, *refs):
    pieces, (window, give, sems) = refs[:-3], refs[-3:]
    n_z = len(pieces) + 1
    pb, z, core = place()
    part = block // 4

    def lanes(chip, index):
        return pl.ds(pl.multiple_of(lax.rem(8 * chip + index, 8 * n_z) * part, 128), part)

    jobs = []
    for e in range(1, n_z):
        to = lax.rem(z - e + n_z, n_z)
        for i in range(3):
            jobs.append((env_ref.at[:, lanes(to, 3 * pb + i)], pieces[e - 1].at[:, i * part : (i + 1) * part]))
    for i in range(12):
        jobs.append((env_ref.at[:, lanes(z, i)], window.at[:, i * part : (i + 1) * part]))
    jobs.append((coupling_ref.at[1 - core], give))
    copies = [pltpu.make_async_copy(src, dst, sems.at[i]) for i, (src, dst) in enumerate(jobs)]
    for copy in copies:
        copy.start()
    for copy in copies:
        copy.wait()


def cut(envelopes, coupling, n_z, block):
    rows = envelopes.shape[0]
    shape = functools.partial(jax.ShapeDtypeStruct, dtype=BF16)
    outs = [shape((rows, 3 * block // 4))] * (n_z - 1) + [shape((rows, 3 * block)), shape(coupling.shape[1:])]
    return pl.pallas_call(
        functools.partial(cut_kernel, block),
        in_specs=[pl.BlockSpec(memory_space=pl.ANY)] * 2,
        out_specs=[pl.BlockSpec(memory_space=pltpu.VMEM)] * len(outs),
        out_shape=outs,
        scratch_shapes=[pltpu.SemaphoreType.DMA((3 * n_z + 10,))],
        name="cut",
    )(envelopes, coupling)


def prep_kernel(block_lines, lines_all, for_other, direct, kq_ref, *refs):
    ins, (out_ref, window) = refs[:-2], refs[-2:]
    pb, _, core = place()
    q = 1 - core if for_other else core
    base, image, turn = turns_of(kq_ref, q, block_lines, lines_all)
    if len(ins) == 1:
        window = ins[0]
    else:
        for rel, src in zip((0, 1, 2, 3) if direct else (0, 1 + core, 2 - core, 3), ins):
            size = src.shape[1]
            window[:, pl.ds(pl.multiple_of((pb ^ rel) * size, 128), size)] = src[...]
    for line in range(2 * block_lines):
        to = slice(line * LINE, (line + 1) * LINE)
        out_ref[0, :, to] = window[:, pl.ds(pl.multiple_of((base + line) * LINE, 128), LINE)]
        shifted = window[:, pl.ds(pl.multiple_of((image + line) * LINE, 128), LINE)].astype(F32)
        out_ref[1, :, to] = pltpu.roll(shifted, turn, 1).astype(BF16)


def prepare(kq_map, ins, block, lines_all, for_other, direct):
    rows = ins[0].shape[0]
    return pl.pallas_call(
        functools.partial(prep_kernel, block // LINE, lines_all, for_other, direct),
        in_specs=[pl.BlockSpec(memory_space=pltpu.SMEM)] + [pl.BlockSpec(memory_space=pltpu.VMEM)] * len(ins),
        out_specs=pl.BlockSpec(memory_space=pltpu.VMEM),
        out_shape=jax.ShapeDtypeStruct((2, rows, 2 * block), BF16),
        scratch_shapes=[pltpu.VMEM((rows, 3 * block), BF16)],
        compiler_params=pltpu.CompilerParams(vmem_limit_bytes=16 << 20),
        name="prepare_other" if for_other else "prepare_own",
    )(kq_map, *ins)


def main_kernel(sources, first, branches, factor, x_ref, *refs):
    amps, (mine_ref, *sends, total, mask) = refs[:sources], refs[sources:]
    shape = mask.shape
    same = lax.broadcasted_iota(jnp.int32, shape, 0) // BANDS == lax.broadcasted_iota(jnp.int32, shape, 1) // BANDS
    mask[...] = same.astype(F32).astype(BF16)
    for line in range(x_ref.shape[2] // LINE):
        to = slice(line * LINE, (line + 1) * LINE)
        for branch in range(branches):
            parts = []
            for tile in range(LINE // 256):
                lanes = slice(line * LINE + tile * 256, line * LINE + (tile + 1) * 256)
                matrix = jnp.concatenate([x_ref[first + branch, :, lanes]] * 16, axis=0) * mask[...]
                own = jnp.concatenate([ref[0, :, lanes] for ref in amps], axis=0)
                parts.append(contract(own, matrix, 1, 0).astype(BF16))
            shifted = jnp.concatenate([ref[1, :, to] for ref in amps], axis=0)
            part = contract(shifted, jnp.concatenate(parts, axis=1), 1, 1)
            total[branch] = part if line == 0 else total[branch] + part
    _, z, core = place()
    states = total.shape[2]
    rows = states // sources
    col = lax.broadcasted_iota(jnp.int32, (states, states), 0)
    target = lax.broadcasted_iota(jnp.int32, (states, states), 1)
    source = lax.rem(col // rows + 2 * z, sources)
    home = (source // 2 * 2 + (source % 2 ^ core)) * rows + col % rows
    to_home = (home == target).astype(F32).astype(BF16)
    for branch in range(branches):
        value = total[branch] * factor
        high = value.astype(BF16)
        moved = contract(high, to_home, 1, 0)
        rest = value[: 2 * rows] - high[: 2 * rows].astype(F32)
        middle = rest.astype(BF16)
        low = (rest - middle.astype(F32)).astype(BF16)
        mine_ref[branch] = moved[: 2 * rows] + contract(middle, to_home, 1, 0) + contract(low, to_home, 1, 0)
        for chip, send in enumerate(sends, 1):
            send[branch] = moved[chip * 2 * rows : (chip + 1) * 2 * rows].astype(BF16)


def products(x, amps, first, branches, factor):
    sources, rows = len(amps), amps[0].shape[1]
    states, width = sources * rows, x.shape[2]
    shape = (branches, 2 * rows, states)
    return pl.pallas_call(
        functools.partial(main_kernel, sources, first, branches, factor),
        in_specs=[pl.BlockSpec(memory_space=pltpu.VMEM)] * (1 + sources),
        out_specs=[pl.BlockSpec(memory_space=pltpu.VMEM)] * (sources // 2),
        out_shape=[jax.ShapeDtypeStruct(shape, F32 if i == 0 else BF16) for i in range(sources // 2)],
        scratch_shapes=[pltpu.VMEM((branches, states, states), F32), pltpu.VMEM((256, 256), BF16)],
        compiler_params=pltpu.CompilerParams(vmem_limit_bytes=32 << 20),
        cost_estimate=pl.CostEstimate(
            flops=4 * branches * states * states * width, bytes_accessed=4 * states * width, transcendentals=0
        ),
        name="products",
    )(x, *amps)


def iota(shape, dim):
    return lax.broadcasted_iota(jnp.int32, shape, dim)


def spread_kernel(_, out_ref):
    _, rows, lanes = out_ref.shape
    row, lane = iota((rows, lanes), 0), iota((rows, lanes), 1)
    here = row % (rows // 4) == lane // BANDS
    index = row // (rows // 4)
    out_ref[0] = (here & (index == lane % 4)).astype(F32).astype(BF16)
    out_ref[1] = (here & (index == lane % BANDS // 4)).astype(F32).astype(BF16)


def spread_matrices(size, earlier):
    return pl.pallas_call(
        spread_kernel,
        in_specs=[pl.BlockSpec(memory_space=pl.ANY)],
        out_specs=pl.BlockSpec(memory_space=pltpu.VMEM),
        out_shape=jax.ShapeDtypeStruct((2, 4 * size, size * BANDS), BF16),
        compiler_params=pltpu.CompilerParams(vmem_limit_bytes=24 << 20),
        cost_estimate=pl.CostEstimate(flops=3 * 10**9, bytes_accessed=10**6, transcendentals=0),
        name="spread",
    )(earlier)


def band_kernel(block_lines, lines_all, kq_ref, spread, coupling_ref, other_ref, next_ref, x_ref):
    branches, _, count = other_ref.shape
    half = BANDS // 4
    size = spread.shape[1] // 4
    shape = (8 * BANDS, 32)
    row, col = iota(shape, 0), iota(shape, 1)
    term, v, c = row // BANDS, row % BANDS // half, row % half
    choice = jnp.where(term < 4, 4 * term + c, 16 + 4 * v + (term - 4))
    pick = (choice == col).astype(F32).astype(BF16)
    shape = (branches * BANDS, size * BANDS)
    row, lane = iota(shape, 0) % BANDS, iota(shape, 1) % BANDS
    keep_cond = (row // half == lane // half).astype(F32)
    keep_val = (row % half == lane % half).astype(F32)
    _, _, core = place()
    base, _, _ = turns_of(kq_ref, core, block_lines, lines_all)
    late = jnp.where(base > 0, 1, 0)
    for part in range(2):
        block = part + late
        terms = []
        for branch in range(branches):
            table = jnp.where(block == core, coupling_ref[core, branch], other_ref[branch])
            table = jnp.where(block == 2, next_ref[branch], table)
            terms.append(contract(pick, table, 1, 0).astype(BF16))
        for start in range(0, count, size):
            width = min(size, count - start)
            lanes = width * BANDS
            values = []
            for kind in range(2):
                rows = []
                for term in terms:
                    slabs = []
                    for index in range(4):
                        at = (4 * kind + index) * BANDS
                        slab = term[at : at + BANDS, start : start + width]
                        if width < size:
                            slab = jnp.concatenate([slab, jnp.zeros((BANDS, size - width), BF16)], axis=1)
                        slabs.append(slab)
                    rows.append(jnp.concatenate(slabs, axis=1))
                values.append(contract(jnp.concatenate(rows, axis=0), spread[kind, :, :lanes], 1, 0))
            total = (values[0] * keep_cond[:, :lanes] - values[1] * keep_val[:, :lanes]).astype(BF16)
            at = (part * count + start) * BANDS
            for branch in range(branches):
                x_ref[branch, :, at : at + lanes] = total[branch * BANDS : (branch + 1) * BANDS]


def band_matrices(kq_map, spread, coupling, other, following, lines_all):
    branches, _, count = other.shape
    return pl.pallas_call(
        functools.partial(band_kernel, count // KY, lines_all),
        in_specs=[pl.BlockSpec(memory_space=pltpu.SMEM)] + [pl.BlockSpec(memory_space=pltpu.VMEM)] * 4,
        out_specs=pl.BlockSpec(memory_space=pltpu.VMEM),
        out_shape=jax.ShapeDtypeStruct((branches, BANDS, 2 * count * BANDS), BF16),
        compiler_params=pltpu.CompilerParams(vmem_limit_bytes=32 << 20),
        cost_estimate=pl.CostEstimate(flops=3 * 10**9, bytes_accessed=10**6, transcendentals=0),
        name="band_matrices",
    )(kq_map, spread, coupling, other, following)


def shards(envelopes, coupling, kq_map):
    n_pb, n_ka = lax.axis_size("pb"), lax.axis_size("ka")
    assert n_pb == 4 and n_ka % 2 == 0 and coupling.shape[0] == 2
    n_z = n_ka // 2
    rows, width = envelopes.shape
    block = width // n_ka
    lines_all = width // LINE
    branches = coupling.shape[1]
    core = lax.axis_index("ka") % 2

    def permute(x, to):
        pairs = []
        for p in range(n_pb):
            for k in range(n_ka):
                tp, tz, tc = to(p, k // 2, k % 2)
                pairs.append((p * n_ka + k, tp * n_ka + (tz % n_z) * 2 + tc))
        return lax.ppermute(x, ("pb", "ka"), pairs)

    def sibling(x):
        return permute(x, lambda p, zz, c: (p, zz, 1 - c))

    def passed_down(e):
        return lambda x: permute(x, lambda p, zz, c: (p, zz - e, c))

    def passed_down(x, e):
        return permute(x, lambda p, zz, c: (p, zz - e, c))

    def prepared(ins, for_other, direct=False):
        return prepare(kq_map, ins, block, lines_all, for_other, direct)

    def after(x, *others):
        return lax.optimization_barrier((x, *others))[0]

    near = sorted({1, n_z - 1})
    far = [e for e in range(2, n_z - 1)]
    *pieces, window, give = cut(envelopes, coupling, n_z, block)
    arrived = {e: passed_down(pieces[e - 1], e) for e in near}
    other_table = sibling(give)
    first_table = jnp.where(core == 0, lax.dynamic_index_in_dim(coupling, core, 0, keepdims=False), other_table)
    next_table = passed_down(first_table, 1)
    pass_on = prepared([after(window, first_table)], True)
    keep = prepared([after(window, pass_on)], False)
    for e in far:
        arrived[e] = passed_down(after(pieces[e - 1], keep), e)
    spread = spread_matrices(min(coupling.shape[3], 128), keep)
    amps = {0: (keep, sibling(pass_on))}

    parts, first_steps = {}, []
    for e in near:
        piece = arrived[e]
        one = permute(piece, lambda p, zz, c: (p ^ (1 + c), zz, c))
        two = permute(piece, lambda p, zz, c: (p ^ (2 - c), zz, c))
        first_steps += [one, two]
        parts[e] = [piece, one, two, permute(one, lambda p, zz, c: (p ^ (2 - c), zz, c))]
    for e in far:
        piece = after(arrived[e], next_table, *first_steps)
        parts[e] = [piece] + [permute(piece, lambda p, zz, c: (p ^ i, zz, c)) for i in (1, 2, 3)]
    late = [parts[e][0] for e in far]
    x = band_matrices(kq_map, spread, coupling, other_table, after(next_table, *late), lines_all)
    for e in near + far:
        piece, *others = parts[e]
        pass_on = prepared([after(piece, x)] + others, True, e in far)
        keep = prepared([after(piece, pass_on)] + others, False, e in far)
        amps[e] = (keep, sibling(pass_on))
    amps = [half for e in range(n_z) for half in amps[e]]

    factor = 1.0 / math.sqrt(float(width))
    edges = [0] + [edge * branches // 9 for edge in GROUPS] + [branches]
    received, mine, other = [], [], []
    for lo, hi in zip(edges[:-1], edges[1:]):
        if len(received) >= 2:
            x, received[-2] = lax.optimization_barrier((x, received[-2]))
        own, *sends = products(x, amps, lo, hi - lo, factor)
        x, own = lax.optimization_barrier((x, own))
        if received:
            own, received[-1] = lax.optimization_barrier((own, received[-1]))
        received.append([own] + [permute(p, lambda p, zz, c: (p, zz + e, c)) for e, p in enumerate(sends, 1)])
    for parts in received:
        total = parts[0]
        for part in parts[1:]:
            total = total + part.astype(F32)
        mine.append(total[:, :rows])
        other.append(sibling(total[:, rows:]))
    mine, other = jnp.concatenate(mine, axis=0), jnp.concatenate(other, axis=0)
    return jnp.where(core == 0, jnp.stack([mine, other]), jnp.stack([other, mine]))


def solution(mesh):
    return jax.shard_map(
        shards,
        mesh=mesh,
        in_specs=(P("ka", None), P("pb", None, None, "ka"), P("pb", "ka")),
        out_specs=P("pb", None, "ka", None),
        check_vma=False,
    )
```

```python
import functools
import math

import jax
import jax.numpy as jnp
from jax import lax
from jax.experimental import pallas as pl
from jax.experimental.pallas import tpu as pltpu
from jax.sharding import PartitionSpec as P

KY = 96
BANDS = 16
LINE = KY * BANDS
GROUPS = (5, 8)
F32 = jnp.float32
SMALL = pl.CostEstimate(flops=1, bytes_accessed=1, transcendentals=0)
BF16 = jnp.bfloat16


def contract(a, b, dim_a, dim_b):
    return lax.dot_general(a, b, (((dim_a,), (dim_b,)), ((), ())), preferred_element_type=F32)


def place():
    ka = lax.axis_index("ka")
    return lax.axis_index("pb"), ka // 2, ka % 2


def turns_of(kq_ref, q, block_lines, lines_all):
    _, z, core = place()
    origin = kq_ref[q, 0]
    step = lax.rem(origin // KY - (2 * z + core) * block_lines + block_lines + lines_all, lines_all) - block_lines
    base = jnp.where(step < 0, block_lines, 0)
    return base, base + step, lax.rem(LINE - lax.rem(origin, KY) * BANDS, LINE)


def cut_kernel(block, env_ref, coupling_ref, *refs):
    pieces, (window, give, sems) = refs[:-3], refs[-3:]
    n_z = len(pieces) + 1
    pb, z, core = place()
    part = block // 4

    def lanes(chip, index):
        return pl.ds(pl.multiple_of(lax.rem(8 * chip + index, 8 * n_z) * part, 128), part)

    jobs = []
    for e in range(1, n_z):
        to = lax.rem(z - e + n_z, n_z)
        for i in range(3):
            jobs.append((env_ref.at[:, lanes(to, 3 * pb + i)], pieces[e - 1].at[:, i * part : (i + 1) * part]))
    for i in range(12):
        jobs.append((env_ref.at[:, lanes(z, i)], window.at[:, i * part : (i + 1) * part]))
    jobs.append((coupling_ref.at[1 - core], give))
    copies = [pltpu.make_async_copy(src, dst, sems.at[i]) for i, (src, dst) in enumerate(jobs)]
    for copy in copies:
        copy.start()
    for copy in copies:
        copy.wait()


def cut(envelopes, coupling, n_z, block):
    rows = envelopes.shape[0]
    shape = functools.partial(jax.ShapeDtypeStruct, dtype=BF16)
    outs = [shape((rows, 3 * block // 4))] * (n_z - 1) + [shape((rows, 3 * block)), shape(coupling.shape[1:])]
    return pl.pallas_call(
        functools.partial(cut_kernel, block),
        in_specs=[pl.BlockSpec(memory_space=pl.ANY)] * 2,
        out_specs=[pl.BlockSpec(memory_space=pltpu.VMEM)] * len(outs),
        out_shape=outs,
        scratch_shapes=[pltpu.SemaphoreType.DMA((3 * n_z + 10,))],
        cost_estimate=SMALL,
        name="cut",
    )(envelopes, coupling)


def prep_kernel(block_lines, lines_all, for_other, direct, kq_ref, *refs):
    ins, (out_ref, window) = refs[:-2], refs[-2:]
    pb, _, core = place()
    q = 1 - core if for_other else core
    base, image, turn = turns_of(kq_ref, q, block_lines, lines_all)
    if len(ins) == 1:
        window = ins[0]
    else:
        for rel, src in zip((0, 1, 2, 3) if direct else (0, 1 + core, 2 - core, 3), ins):
            size = src.shape[1]
            window[:, pl.ds(pl.multiple_of((pb ^ rel) * size, 128), size)] = src[...]
    for line in range(2 * block_lines):
        to = slice(line * LINE, (line + 1) * LINE)
        out_ref[0, :, to] = window[:, pl.ds(pl.multiple_of((base + line) * LINE, 128), LINE)]
        shifted = window[:, pl.ds(pl.multiple_of((image + line) * LINE, 128), LINE)].astype(F32)
        out_ref[1, :, to] = pltpu.roll(shifted, turn, 1).astype(BF16)


def prepare(kq_map, ins, block, lines_all, for_other, direct):
    rows = ins[0].shape[0]
    return pl.pallas_call(
        functools.partial(prep_kernel, block // LINE, lines_all, for_other, direct),
        in_specs=[pl.BlockSpec(memory_space=pltpu.SMEM)] + [pl.BlockSpec(memory_space=pltpu.VMEM)] * len(ins),
        out_specs=pl.BlockSpec(memory_space=pltpu.VMEM),
        out_shape=jax.ShapeDtypeStruct((2, rows, 2 * block), BF16),
        scratch_shapes=[pltpu.VMEM((rows, 3 * block), BF16)],
        compiler_params=pltpu.CompilerParams(vmem_limit_bytes=16 << 20),
        cost_estimate=SMALL,
        name="prepare_other" if for_other else "prepare_own",
    )(kq_map, *ins)


def main_kernel(sources, first, branches, factor, x_ref, *refs):
    amps, (mine_ref, *sends, total, mask) = refs[:sources], refs[sources:]
    shape = mask.shape
    same = lax.broadcasted_iota(jnp.int32, shape, 0) // BANDS == lax.broadcasted_iota(jnp.int32, shape, 1) // BANDS
    mask[...] = same.astype(F32).astype(BF16)
    for line in range(x_ref.shape[2] // LINE):
        to = slice(line * LINE, (line + 1) * LINE)
        for branch in range(branches):
            parts = []
            for tile in range(LINE // 256):
                lanes = slice(line * LINE + tile * 256, line * LINE + (tile + 1) * 256)
                matrix = jnp.concatenate([x_ref[first + branch, :, lanes]] * 16, axis=0) * mask[...]
                own = jnp.concatenate([ref[0, :, lanes] for ref in amps], axis=0)
                parts.append(contract(own, matrix, 1, 0).astype(BF16))
            shifted = jnp.concatenate([ref[1, :, to] for ref in amps], axis=0)
            part = contract(shifted, jnp.concatenate(parts, axis=1), 1, 1)
            total[branch] = part if line == 0 else total[branch] + part
    _, z, core = place()
    states = total.shape[2]
    rows = states // sources
    col = lax.broadcasted_iota(jnp.int32, (states, states), 0)
    target = lax.broadcasted_iota(jnp.int32, (states, states), 1)
    source = lax.rem(col // rows + 2 * z, sources)
    home = (source // 2 * 2 + (source % 2 ^ core)) * rows + col % rows
    to_home = (home == target).astype(F32).astype(BF16)
    for branch in range(branches):
        value = total[branch] * factor
        high = value.astype(BF16)
        moved = contract(high, to_home, 1, 0)
        rest = value[: 2 * rows] - high[: 2 * rows].astype(F32)
        middle = rest.astype(BF16)
        low = (rest - middle.astype(F32)).astype(BF16)
        mine_ref[branch] = moved[: 2 * rows] + contract(middle, to_home, 1, 0) + contract(low, to_home, 1, 0)
        for chip, send in enumerate(sends, 1):
            send[branch] = moved[chip * 2 * rows : (chip + 1) * 2 * rows].astype(BF16)


def products(x, amps, first, branches, factor):
    sources, rows = len(amps), amps[0].shape[1]
    states, width = sources * rows, x.shape[2]
    shape = (branches, 2 * rows, states)
    return pl.pallas_call(
        functools.partial(main_kernel, sources, first, branches, factor),
        in_specs=[pl.BlockSpec(memory_space=pltpu.VMEM)] * (1 + sources),
        out_specs=[pl.BlockSpec(memory_space=pltpu.VMEM)] * (sources // 2),
        out_shape=[jax.ShapeDtypeStruct(shape, F32 if i == 0 else BF16) for i in range(sources // 2)],
        scratch_shapes=[pltpu.VMEM((branches, states, states), F32), pltpu.VMEM((256, 256), BF16)],
        compiler_params=pltpu.CompilerParams(vmem_limit_bytes=32 << 20),
        cost_estimate=pl.CostEstimate(
            flops=4 * branches * states * states * width, bytes_accessed=4 * states * width, transcendentals=0
        ),
        name="products",
    )(x, *amps)


def iota(shape, dim):
    return lax.broadcasted_iota(jnp.int32, shape, dim)


def spread_kernel(_, out_ref):
    _, rows, lanes = out_ref.shape
    row, lane = iota((rows, lanes), 0), iota((rows, lanes), 1)
    here = row % (rows // 4) == lane // BANDS
    index = row // (rows // 4)
    out_ref[0] = (here & (index == lane % 4)).astype(F32).astype(BF16)
    out_ref[1] = (here & (index == lane % BANDS // 4)).astype(F32).astype(BF16)


def spread_matrices(size, earlier):
    return pl.pallas_call(
        spread_kernel,
        in_specs=[pl.BlockSpec(memory_space=pl.ANY)],
        out_specs=pl.BlockSpec(memory_space=pltpu.VMEM),
        out_shape=jax.ShapeDtypeStruct((2, 4 * size, size * BANDS), BF16),
        compiler_params=pltpu.CompilerParams(vmem_limit_bytes=24 << 20),
        cost_estimate=SMALL,
        name="spread",
    )(earlier)


def band_kernel(block_lines, lines_all, kq_ref, spread, coupling_ref, other_ref, next_ref, x_ref):
    branches, _, count = other_ref.shape
    half = BANDS // 4
    size = spread.shape[1] // 4
    shape = (8 * BANDS, 32)
    row, col = iota(shape, 0), iota(shape, 1)
    term, v, c = row // BANDS, row % BANDS // half, row % half
    choice = jnp.where(term < 4, 4 * term + c, 16 + 4 * v + (term - 4))
    pick = (choice == col).astype(F32).astype(BF16)
    shape = (branches * BANDS, size * BANDS)
    row, lane = iota(shape, 0) % BANDS, iota(shape, 1) % BANDS
    keep_cond = (row // half == lane // half).astype(F32)
    keep_val = (row % half == lane % half).astype(F32)
    _, _, core = place()
    base, _, _ = turns_of(kq_ref, core, block_lines, lines_all)
    late = jnp.where(base > 0, 1, 0)
    for part in range(2):
        block = part + late
        terms = []
        for branch in range(branches):
            table = jnp.where(block == core, coupling_ref[core, branch], other_ref[branch])
            table = jnp.where(block == 2, next_ref[branch], table)
            terms.append(contract(pick, table, 1, 0).astype(BF16))
        for start in range(0, count, size):
            width = min(size, count - start)
            lanes = width * BANDS
            values = []
            for kind in range(2):
                rows = []
                for term in terms:
                    slabs = []
                    for index in range(4):
                        at = (4 * kind + index) * BANDS
                        slab = term[at : at + BANDS, start : start + width]
                        if width < size:
                            slab = jnp.concatenate([slab, jnp.zeros((BANDS, size - width), BF16)], axis=1)
                        slabs.append(slab)
                    rows.append(jnp.concatenate(slabs, axis=1))
                values.append(contract(jnp.concatenate(rows, axis=0), spread[kind, :, :lanes], 1, 0))
            total = (values[0] * keep_cond[:, :lanes] - values[1] * keep_val[:, :lanes]).astype(BF16)
            at = (part * count + start) * BANDS
            for branch in range(branches):
                x_ref[branch, :, at : at + lanes] = total[branch * BANDS : (branch + 1) * BANDS]


def band_matrices(kq_map, spread, coupling, other, following, lines_all):
    branches, _, count = other.shape
    return pl.pallas_call(
        functools.partial(band_kernel, count // KY, lines_all),
        in_specs=[pl.BlockSpec(memory_space=pltpu.SMEM)] + [pl.BlockSpec(memory_space=pltpu.VMEM)] * 4,
        out_specs=pl.BlockSpec(memory_space=pltpu.VMEM),
        out_shape=jax.ShapeDtypeStruct((branches, BANDS, 2 * count * BANDS), BF16),
        compiler_params=pltpu.CompilerParams(vmem_limit_bytes=32 << 20),
        cost_estimate=SMALL,
        name="band_matrices",
    )(kq_map, spread, coupling, other, following)


def shards(envelopes, coupling, kq_map):
    n_pb, n_ka = lax.axis_size("pb"), lax.axis_size("ka")
    assert n_pb == 4 and n_ka % 2 == 0 and coupling.shape[0] == 2
    n_z = n_ka // 2
    rows, width = envelopes.shape
    block = width // n_ka
    lines_all = width // LINE
    branches = coupling.shape[1]
    core = lax.axis_index("ka") % 2

    def permute(x, to):
        pairs = []
        for p in range(n_pb):
            for k in range(n_ka):
                tp, tz, tc = to(p, k // 2, k % 2)
                pairs.append((p * n_ka + k, tp * n_ka + (tz % n_z) * 2 + tc))
        return lax.ppermute(x, ("pb", "ka"), pairs)

    def sibling(x):
        return permute(x, lambda p, zz, c: (p, zz, 1 - c))

    def passed_down(e):
        return lambda x: permute(x, lambda p, zz, c: (p, zz - e, c))

    def passed_down(x, e):
        return permute(x, lambda p, zz, c: (p, zz - e, c))

    def prepared(ins, for_other, direct=False):
        return prepare(kq_map, ins, block, lines_all, for_other, direct)

    def after(x, *others):
        return lax.optimization_barrier((x, *others))[0]

    near = sorted({1, n_z - 1})
    far = [e for e in range(2, n_z - 1)]
    *pieces, window, give = cut(envelopes, coupling, n_z, block)
    arrived = {e: passed_down(pieces[e - 1], e) for e in near}
    pass_on = prepared([window], True)
    keep = prepared([after(window, pass_on)], False)
    for e in far:
        arrived[e] = passed_down(after(pieces[e - 1], keep), e)
    spread = spread_matrices(min(coupling.shape[3], 64), keep)
    amps = {0: (keep, sibling(pass_on))}

    parts, first_steps = {}, []
    for e in near:
        piece = arrived[e]
        one = permute(piece, lambda p, zz, c: (p ^ (1 + c), zz, c))
        two = permute(piece, lambda p, zz, c: (p ^ (2 - c), zz, c))
        three = permute(one, lambda p, zz, c: (p ^ (2 - c), zz, c))
        first_steps += [one, two, three] if e == 1 else [one, two]
        parts[e] = [piece, one, two, three]
    for e in far:
        piece = after(arrived[e], *first_steps)
        parts[e] = [piece] + [permute(piece, lambda p, zz, c: (p ^ i, zz, c)) for i in (1, 2, 3)]
    other_table = sibling(give)
    first_table = jnp.where(core == 0, lax.dynamic_index_in_dim(coupling, core, 0, keepdims=False), other_table)
    next_table = passed_down(after(first_table, *[arrived[e] for e in near[1:]]), 1)
    next_table = after(next_table, *[parts[e][0] for e in far])
    x = band_matrices(kq_map, spread, coupling, other_table, next_table, lines_all)
    for e in near + far:
        piece, *others = parts[e]
        pass_on = prepared([after(piece, x)] + others, True, e in far)
        keep = prepared([after(piece, pass_on)] + others, False, e in far)
        amps[e] = (keep, sibling(pass_on))
    amps = [half for e in range(n_z) for half in amps[e]]

    factor = 1.0 / math.sqrt(float(width))
    edges = [0] + [edge * branches // 9 for edge in GROUPS] + [branches]
    received, mine, other = [], [], []
    for lo, hi in zip(edges[:-1], edges[1:]):
        if len(received) >= 2:
            x, received[-2] = lax.optimization_barrier((x, received[-2]))
        own, *sends = products(x, amps, lo, hi - lo, factor)
        x, own = lax.optimization_barrier((x, own))
        if received:
            own, received[-1] = lax.optimization_barrier((own, received[-1]))
        received.append([own] + [permute(p, lambda p, zz, c: (p, zz + e, c)) for e, p in enumerate(sends, 1)])
    for parts in received:
        total = parts[0]
        for part in parts[1:]:
            total = total + part.astype(F32)
        mine.append(total[:, :rows])
        other.append(sibling(total[:, rows:]))
    mine, other = jnp.concatenate(mine, axis=0), jnp.concatenate(other, axis=0)
    return jnp.where(core == 0, jnp.stack([mine, other]), jnp.stack([other, mine]))


def solution(mesh):
    return jax.shard_map(
        shards,
        mesh=mesh,
        in_specs=(P("ka", None), P("pb", None, None, "ka"), P("pb", "ka")),
        out_specs=P("pb", None, "ka", None),
        check_vma=False,
    )
```

```python
import functools
import math

import jax
import jax.numpy as jnp
from jax import lax
from jax.experimental import pallas as pl
from jax.experimental.pallas import tpu as pltpu
from jax.sharding import PartitionSpec as P

KY = 96
BANDS = 16
LINE = KY * BANDS
GROUPS = (5, 8)
F32 = jnp.float32
SMALL = pl.CostEstimate(flops=1, bytes_accessed=1, transcendentals=0)
BF16 = jnp.bfloat16


def contract(a, b, dim_a, dim_b):
    return lax.dot_general(a, b, (((dim_a,), (dim_b,)), ((), ())), preferred_element_type=F32)


def place():
    ka = lax.axis_index("ka")
    return lax.axis_index("pb"), ka // 2, ka % 2


def turns_of(kq_ref, q, block_lines, lines_all):
    _, z, core = place()
    origin = kq_ref[q, 0]
    step = lax.rem(origin // KY - (2 * z + core) * block_lines + block_lines + lines_all, lines_all) - block_lines
    base = jnp.where(step < 0, block_lines, 0)
    return base, base + step, lax.rem(LINE - lax.rem(origin, KY) * BANDS, LINE)


def cut_kernel(block, env_ref, coupling_ref, *refs):
    pieces, (window, give, sems) = refs[:-3], refs[-3:]
    n_z = len(pieces) + 1
    pb, z, core = place()
    part = block // 4

    def lanes(chip, index):
        return pl.ds(pl.multiple_of(lax.rem(8 * chip + index, 8 * n_z) * part, 128), part)

    jobs = []
    for e in range(1, n_z):
        to = lax.rem(z - e + n_z, n_z)
        for i in range(3):
            jobs.append((env_ref.at[:, lanes(to, 3 * pb + i)], pieces[e - 1].at[:, i * part : (i + 1) * part]))
    for i in range(12):
        jobs.append((env_ref.at[:, lanes(z, i)], window.at[:, i * part : (i + 1) * part]))
    jobs.append((coupling_ref.at[1 - core], give))
    copies = [pltpu.make_async_copy(src, dst, sems.at[i]) for i, (src, dst) in enumerate(jobs)]
    for copy in copies:
        copy.start()
    for copy in copies:
        copy.wait()


def cut(envelopes, coupling, n_z, block):
    rows = envelopes.shape[0]
    shape = functools.partial(jax.ShapeDtypeStruct, dtype=BF16)
    outs = [shape((rows, 3 * block // 4))] * (n_z - 1) + [shape((rows, 3 * block)), shape(coupling.shape[1:])]
    return pl.pallas_call(
        functools.partial(cut_kernel, block),
        in_specs=[pl.BlockSpec(memory_space=pl.ANY)] * 2,
        out_specs=[pl.BlockSpec(memory_space=pltpu.VMEM)] * len(outs),
        out_shape=outs,
        scratch_shapes=[pltpu.SemaphoreType.DMA((3 * n_z + 10,))],
        cost_estimate=SMALL,
        name="cut",
    )(envelopes, coupling)


def prep_kernel(block_lines, lines_all, for_other, direct, kq_ref, *refs):
    ins, (out_ref, window) = refs[:-2], refs[-2:]
    pb, _, core = place()
    q = 1 - core if for_other else core
    base, image, turn = turns_of(kq_ref, q, block_lines, lines_all)
    if len(ins) == 1:
        window = ins[0]
    else:
        for rel, src in zip((0, 1, 2, 3) if direct else (0, 1 + core, 2 - core, 3), ins):
            size = src.shape[1]
            window[:, pl.ds(pl.multiple_of((pb ^ rel) * size, 128), size)] = src[...]
    for line in range(2 * block_lines):
        to = slice(line * LINE, (line + 1) * LINE)
        out_ref[0, :, to] = window[:, pl.ds(pl.multiple_of((base + line) * LINE, 128), LINE)]
        shifted = window[:, pl.ds(pl.multiple_of((image + line) * LINE, 128), LINE)].astype(F32)
        out_ref[1, :, to] = pltpu.roll(shifted, turn, 1).astype(BF16)


def prepare(kq_map, ins, block, lines_all, for_other, direct):
    rows = ins[0].shape[0]
    return pl.pallas_call(
        functools.partial(prep_kernel, block // LINE, lines_all, for_other, direct),
        in_specs=[pl.BlockSpec(memory_space=pltpu.SMEM)] + [pl.BlockSpec(memory_space=pltpu.VMEM)] * len(ins),
        out_specs=pl.BlockSpec(memory_space=pltpu.VMEM),
        out_shape=jax.ShapeDtypeStruct((2, rows, 2 * block), BF16),
        scratch_shapes=[pltpu.VMEM((rows, 3 * block), BF16)],
        compiler_params=pltpu.CompilerParams(vmem_limit_bytes=16 << 20),
        cost_estimate=SMALL,
        name="prepare_other" if for_other else "prepare_own",
    )(kq_map, *ins)


def main_kernel(sources, first, branches, factor, x_ref, *refs):
    amps, (mine_ref, *sends, total, mask) = refs[:sources], refs[sources:]
    shape = mask.shape
    same = lax.broadcasted_iota(jnp.int32, shape, 0) // BANDS == lax.broadcasted_iota(jnp.int32, shape, 1) // BANDS
    mask[...] = same.astype(F32).astype(BF16)
    for line in range(x_ref.shape[2] // LINE):
        to = slice(line * LINE, (line + 1) * LINE)
        for branch in range(branches):
            parts = []
            for tile in range(LINE // 256):
                lanes = slice(line * LINE + tile * 256, line * LINE + (tile + 1) * 256)
                matrix = jnp.concatenate([x_ref[first + branch, :, lanes]] * 16, axis=0) * mask[...]
                own = jnp.concatenate([ref[0, :, lanes] for ref in amps], axis=0)
                parts.append(contract(own, matrix, 1, 0).astype(BF16))
            shifted = jnp.concatenate([ref[1, :, to] for ref in amps], axis=0)
            part = contract(shifted, jnp.concatenate(parts, axis=1), 1, 1)
            total[branch] = part if line == 0 else total[branch] + part
    _, z, core = place()
    states = total.shape[2]
    rows = states // sources
    col = lax.broadcasted_iota(jnp.int32, (states, states), 0)
    target = lax.broadcasted_iota(jnp.int32, (states, states), 1)
    source = lax.rem(col // rows + 2 * z, sources)
    home = (source // 2 * 2 + (source % 2 ^ core)) * rows + col % rows
    to_home = (home == target).astype(F32).astype(BF16)
    for branch in range(branches):
        value = total[branch] * factor
        high = value.astype(BF16)
        moved = contract(high, to_home, 1, 0)
        rest = value[: 2 * rows] - high[: 2 * rows].astype(F32)
        middle = rest.astype(BF16)
        low = (rest - middle.astype(F32)).astype(BF16)
        mine_ref[branch] = moved[: 2 * rows] + contract(middle, to_home, 1, 0) + contract(low, to_home, 1, 0)
        for chip, send in enumerate(sends, 1):
            send[branch] = moved[chip * 2 * rows : (chip + 1) * 2 * rows].astype(BF16)


def products(x, amps, first, branches, factor):
    sources, rows = len(amps), amps[0].shape[1]
    states, width = sources * rows, x.shape[2]
    shape = (branches, 2 * rows, states)
    return pl.pallas_call(
        functools.partial(main_kernel, sources, first, branches, factor),
        in_specs=[pl.BlockSpec(memory_space=pltpu.VMEM)] * (1 + sources),
        out_specs=[pl.BlockSpec(memory_space=pltpu.VMEM)] * (sources // 2),
        out_shape=[jax.ShapeDtypeStruct(shape, F32 if i == 0 else BF16) for i in range(sources // 2)],
        scratch_shapes=[pltpu.VMEM((branches, states, states), F32), pltpu.VMEM((256, 256), BF16)],
        compiler_params=pltpu.CompilerParams(vmem_limit_bytes=32 << 20),
        cost_estimate=pl.CostEstimate(
            flops=4 * branches * states * states * width, bytes_accessed=4 * states * width, transcendentals=0
        ),
        name="products",
    )(x, *amps)


def iota(shape, dim):
    return lax.broadcasted_iota(jnp.int32, shape, dim)


def spread_kernel(_, out_ref):
    _, rows, lanes = out_ref.shape
    row, lane = iota((rows, lanes), 0), iota((rows, lanes), 1)
    here = row % (rows // 4) == lane // BANDS
    index = row // (rows // 4)
    out_ref[0] = (here & (index == lane % 4)).astype(F32).astype(BF16)
    out_ref[1] = (here & (index == lane % BANDS // 4)).astype(F32).astype(BF16)


def spread_matrices(size, earlier):
    return pl.pallas_call(
        spread_kernel,
        in_specs=[pl.BlockSpec(memory_space=pl.ANY)],
        out_specs=pl.BlockSpec(memory_space=pltpu.VMEM),
        out_shape=jax.ShapeDtypeStruct((2, 4 * size, size * BANDS), BF16),
        compiler_params=pltpu.CompilerParams(vmem_limit_bytes=24 << 20),
        cost_estimate=SMALL,
        name="spread",
    )(earlier)


def band_kernel(block_lines, lines_all, kq_ref, spread, coupling_ref, other_ref, next_ref, x_ref):
    branches, _, count = other_ref.shape
    half = BANDS // 4
    size = spread.shape[1] // 4
    shape = (8 * BANDS, 32)
    row, col = iota(shape, 0), iota(shape, 1)
    term, v, c = row // BANDS, row % BANDS // half, row % half
    choice = jnp.where(term < 4, 4 * term + c, 16 + 4 * v + (term - 4))
    pick = (choice == col).astype(F32).astype(BF16)
    shape = (branches * BANDS, size * BANDS)
    row, lane = iota(shape, 0) % BANDS, iota(shape, 1) % BANDS
    keep_cond = (row // half == lane // half).astype(F32)
    keep_val = (row % half == lane % half).astype(F32)
    _, _, core = place()
    base, _, _ = turns_of(kq_ref, core, block_lines, lines_all)
    late = jnp.where(base > 0, 1, 0)
    for part in range(2):
        block = part + late
        terms = []
        for branch in range(branches):
            table = jnp.where(block == core, coupling_ref[core, branch], other_ref[branch])
            table = jnp.where(block == 2, next_ref[branch], table)
            terms.append(contract(pick, table, 1, 0).astype(BF16))
        for start in range(0, count, size):
            width = min(size, count - start)
            lanes = width * BANDS
            values = []
            for kind in range(2):
                rows = []
                for term in terms:
                    slabs = []
                    for index in range(4):
                        at = (4 * kind + index) * BANDS
                        slab = term[at : at + BANDS, start : start + width]
                        if width < size:
                            slab = jnp.concatenate([slab, jnp.zeros((BANDS, size - width), BF16)], axis=1)
                        slabs.append(slab)
                    rows.append(jnp.concatenate(slabs, axis=1))
                values.append(contract(jnp.concatenate(rows, axis=0), spread[kind, :, :lanes], 1, 0))
            total = (values[0] * keep_cond[:, :lanes] - values[1] * keep_val[:, :lanes]).astype(BF16)
            at = (part * count + start) * BANDS
            for branch in range(branches):
                x_ref[branch, :, at : at + lanes] = total[branch * BANDS : (branch + 1) * BANDS]


def band_matrices(kq_map, spread, coupling, other, following, lines_all):
    branches, _, count = other.shape
    return pl.pallas_call(
        functools.partial(band_kernel, count // KY, lines_all),
        in_specs=[pl.BlockSpec(memory_space=pltpu.SMEM)] + [pl.BlockSpec(memory_space=pltpu.VMEM)] * 4,
        out_specs=pl.BlockSpec(memory_space=pltpu.VMEM),
        out_shape=jax.ShapeDtypeStruct((branches, BANDS, 2 * count * BANDS), BF16),
        compiler_params=pltpu.CompilerParams(vmem_limit_bytes=32 << 20),
        cost_estimate=SMALL,
        name="band_matrices",
    )(kq_map, spread, coupling, other, following)


def shards(envelopes, coupling, kq_map):
    n_pb, n_ka = lax.axis_size("pb"), lax.axis_size("ka")
    assert n_pb == 4 and n_ka % 2 == 0 and coupling.shape[0] == 2
    n_z = n_ka // 2
    rows, width = envelopes.shape
    block = width // n_ka
    lines_all = width // LINE
    branches = coupling.shape[1]
    core = lax.axis_index("ka") % 2

    def permute(x, to):
        pairs = []
        for p in range(n_pb):
            for k in range(n_ka):
                tp, tz, tc = to(p, k // 2, k % 2)
                pairs.append((p * n_ka + k, tp * n_ka + (tz % n_z) * 2 + tc))
        return lax.ppermute(x, ("pb", "ka"), pairs)

    def sibling(x):
        return permute(x, lambda p, zz, c: (p, zz, 1 - c))

    def passed_down(e):
        return lambda x: permute(x, lambda p, zz, c: (p, zz - e, c))

    def passed_down(x, e):
        return permute(x, lambda p, zz, c: (p, zz - e, c))

    def prepared(ins, for_other, direct=False):
        return prepare(kq_map, ins, block, lines_all, for_other, direct)

    def after(x, *others):
        return lax.optimization_barrier((x, *others))[0]

    near = sorted({1, n_z - 1})
    far = [e for e in range(2, n_z - 1)]
    *pieces, window, give = cut(envelopes, coupling, n_z, block)
    arrived = {e: passed_down(pieces[e - 1], e) for e in near}
    pass_on = prepared([window], True)
    keep = prepared([after(window, pass_on)], False)
    for e in far:
        arrived[e] = passed_down(after(pieces[e - 1], keep), e)
    spread = spread_matrices(min(coupling.shape[3], 64), keep)
    amps = {0: (keep, sibling(pass_on))}

    other_table = sibling(give)
    first_table = jnp.where(core == 0, lax.dynamic_index_in_dim(coupling, core, 0, keepdims=False), other_table)
    next_table = passed_down(first_table, 1)

    parts, first_steps = {}, []
    for e in near:
        piece = arrived[e]
        one = permute(piece, lambda p, zz, c: (p ^ (1 + c), zz, c))
        two = permute(piece, lambda p, zz, c: (p ^ (2 - c), zz, c))
        if e == 1:
            one = after(one, next_table)
        three = permute(one, lambda p, zz, c: (p ^ (2 - c), zz, c))
        first_steps += [one, two]
        parts[e] = [piece, one, two, three]
    for e in far:
        piece = after(arrived[e], next_table, *first_steps)
        parts[e] = [piece] + [permute(piece, lambda p, zz, c: (p ^ i, zz, c)) for i in (1, 2, 3)]
    x = band_matrices(kq_map, spread, coupling, other_table, after(next_table, *[parts[e][0] for e in far]), lines_all)
    for e in near + far:
        piece, *others = parts[e]
        done = [x] if e in near else [x, amps[1][0]]
        pass_on = prepared([after(piece, *done)] + others, True, e in far)
        keep = prepared([after(piece, pass_on)] + others, False, e in far)
        amps[e] = (keep, sibling(pass_on))
    amps = [half for e in range(n_z) for half in amps[e]]

    factor = 1.0 / math.sqrt(float(width))
    edges = [0] + [edge * branches // 9 for edge in GROUPS] + [branches]
    received, mine, other = [], [], []
    for lo, hi in zip(edges[:-1], edges[1:]):
        if len(received) >= 2:
            x, received[-2] = lax.optimization_barrier((x, received[-2]))
        own, *sends = products(x, amps, lo, hi - lo, factor)
        x, own = lax.optimization_barrier((x, own))
        if received:
            own, received[-1] = lax.optimization_barrier((own, received[-1]))
        received.append([own] + [permute(p, lambda p, zz, c: (p, zz + e, c)) for e, p in enumerate(sends, 1)])
    for parts in received:
        total = parts[0]
        for part in parts[1:]:
            total = total + part.astype(F32)
        mine.append(total[:, :rows])
        other.append(sibling(total[:, rows:]))
    mine, other = jnp.concatenate(mine, axis=0), jnp.concatenate(other, axis=0)
    return jnp.where(core == 0, jnp.stack([mine, other]), jnp.stack([other, mine]))


def solution(mesh):
    return jax.shard_map(
        shards,
        mesh=mesh,
        in_specs=(P("ka", None), P("pb", None, None, "ka"), P("pb", "ka")),
        out_specs=P("pb", None, "ka", None),
        check_vma=False,
    )
```

```python
import functools
import math

import jax
import jax.numpy as jnp
from jax import lax
from jax.experimental import pallas as pl
from jax.experimental.pallas import tpu as pltpu
from jax.sharding import PartitionSpec as P

KY = 96
BANDS = 16
LINE = KY * BANDS
GROUPS = (4, 8)
F32 = jnp.float32
SMALL = pl.CostEstimate(flops=1, bytes_accessed=1, transcendentals=0)
BF16 = jnp.bfloat16


def contract(a, b, dim_a, dim_b):
    return lax.dot_general(a, b, (((dim_a,), (dim_b,)), ((), ())), preferred_element_type=F32)


def place():
    ka = lax.axis_index("ka")
    return lax.axis_index("pb"), ka // 2, ka % 2


def turns_of(kq_ref, q, block_lines, lines_all):
    _, z, core = place()
    origin = kq_ref[q, 0]
    step = lax.rem(origin // KY - (2 * z + core) * block_lines + block_lines + lines_all, lines_all) - block_lines
    base = jnp.where(step < 0, block_lines, 0)
    return base, base + step, lax.rem(LINE - lax.rem(origin, KY) * BANDS, LINE)


def cut_kernel(block, env_ref, coupling_ref, *refs):
    pieces, (window, give, sems) = refs[:-3], refs[-3:]
    n_z = len(pieces) + 1
    pb, z, core = place()
    part = block // 4

    def lanes(chip, index):
        return pl.ds(pl.multiple_of(lax.rem(8 * chip + index, 8 * n_z) * part, 128), part)

    jobs = []
    for e in range(1, n_z):
        to = lax.rem(z - e + n_z, n_z)
        for i in range(3):
            jobs.append((env_ref.at[:, lanes(to, 3 * pb + i)], pieces[e - 1].at[:, i * part : (i + 1) * part]))
    for i in range(12):
        jobs.append((env_ref.at[:, lanes(z, i)], window.at[:, i * part : (i + 1) * part]))
    jobs.append((coupling_ref.at[1 - core], give))
    copies = [pltpu.make_async_copy(src, dst, sems.at[i]) for i, (src, dst) in enumerate(jobs)]
    for copy in copies:
        copy.start()
    for copy in copies:
        copy.wait()


def cut(envelopes, coupling, n_z, block):
    rows = envelopes.shape[0]
    shape = functools.partial(jax.ShapeDtypeStruct, dtype=BF16)
    outs = [shape((rows, 3 * block // 4))] * (n_z - 1) + [shape((rows, 3 * block)), shape(coupling.shape[1:])]
    return pl.pallas_call(
        functools.partial(cut_kernel, block),
        in_specs=[pl.BlockSpec(memory_space=pl.ANY)] * 2,
        out_specs=[pl.BlockSpec(memory_space=pltpu.VMEM)] * len(outs),
        out_shape=outs,
        scratch_shapes=[pltpu.SemaphoreType.DMA((3 * n_z + 10,))],
        cost_estimate=SMALL,
        name="cut",
    )(envelopes, coupling)


def prep_kernel(block_lines, lines_all, for_other, direct, kq_ref, *refs):
    ins, (out_ref, window) = refs[:-2], refs[-2:]
    pb, _, core = place()
    q = 1 - core if for_other else core
    base, image, turn = turns_of(kq_ref, q, block_lines, lines_all)
    if len(ins) == 1:
        window = ins[0]
    else:
        for rel, src in zip((0, 1, 2, 3) if direct else (0, 1 + core, 2 - core, 3), ins):
            size = src.shape[1]
            window[:, pl.ds(pl.multiple_of((pb ^ rel) * size, 128), size)] = src[...]
    for line in range(2 * block_lines):
        to = slice(line * LINE, (line + 1) * LINE)
        out_ref[0, :, to] = window[:, pl.ds(pl.multiple_of((base + line) * LINE, 128), LINE)]
        shifted = window[:, pl.ds(pl.multiple_of((image + line) * LINE, 128), LINE)].astype(F32)
        out_ref[1, :, to] = pltpu.roll(shifted, turn, 1).astype(BF16)


def prepare(kq_map, ins, block, lines_all, for_other, direct):
    rows = ins[0].shape[0]
    return pl.pallas_call(
        functools.partial(prep_kernel, block // LINE, lines_all, for_other, direct),
        in_specs=[pl.BlockSpec(memory_space=pltpu.SMEM)] + [pl.BlockSpec(memory_space=pltpu.VMEM)] * len(ins),
        out_specs=pl.BlockSpec(memory_space=pltpu.VMEM),
        out_shape=jax.ShapeDtypeStruct((2, rows, 2 * block), BF16),
        scratch_shapes=[pltpu.VMEM((rows, 3 * block), BF16)],
        compiler_params=pltpu.CompilerParams(vmem_limit_bytes=16 << 20),
        cost_estimate=SMALL,
        name="prepare_other" if for_other else "prepare_own",
    )(kq_map, *ins)


def main_kernel(sources, first, branches, factor, x_ref, *refs):
    amps, (mine_ref, *sends, total, mask) = refs[:sources], refs[sources:]
    shape = mask.shape
    same = lax.broadcasted_iota(jnp.int32, shape, 0) // BANDS == lax.broadcasted_iota(jnp.int32, shape, 1) // BANDS
    mask[...] = same.astype(F32).astype(BF16)
    for line in range(x_ref.shape[2] // LINE):
        to = slice(line * LINE, (line + 1) * LINE)
        for branch in range(branches):
            parts = []
            for tile in range(LINE // 256):
                lanes = slice(line * LINE + tile * 256, line * LINE + (tile + 1) * 256)
                matrix = jnp.concatenate([x_ref[first + branch, :, lanes]] * 16, axis=0) * mask[...]
                own = jnp.concatenate([ref[0, :, lanes] for ref in amps], axis=0)
                parts.append(contract(own, matrix, 1, 0).astype(BF16))
            shifted = jnp.concatenate([ref[1, :, to] for ref in amps], axis=0)
            part = contract(shifted, jnp.concatenate(parts, axis=1), 1, 1)
            total[branch] = part if line == 0 else total[branch] + part
    _, z, core = place()
    states = total.shape[2]
    rows = states // sources
    col = lax.broadcasted_iota(jnp.int32, (states, states), 0)
    target = lax.broadcasted_iota(jnp.int32, (states, states), 1)
    source = lax.rem(col // rows + 2 * z, sources)
    home = (source // 2 * 2 + (source % 2 ^ core)) * rows + col % rows
    to_home = (home == target).astype(F32).astype(BF16)
    for branch in range(branches):
        value = total[branch] * factor
        high = value.astype(BF16)
        moved = contract(high, to_home, 1, 0)
        rest = value[: 2 * rows] - high[: 2 * rows].astype(F32)
        middle = rest.astype(BF16)
        low = (rest - middle.astype(F32)).astype(BF16)
        mine_ref[branch] = moved[: 2 * rows] + contract(middle, to_home, 1, 0) + contract(low, to_home, 1, 0)
        for chip, send in enumerate(sends, 1):
            send[branch] = moved[chip * 2 * rows : (chip + 1) * 2 * rows].astype(BF16)


def products(x, amps, first, branches, factor):
    sources, rows = len(amps), amps[0].shape[1]
    states, width = sources * rows, x.shape[2]
    shape = (branches, 2 * rows, states)
    return pl.pallas_call(
        functools.partial(main_kernel, sources, first, branches, factor),
        in_specs=[pl.BlockSpec(memory_space=pltpu.VMEM)] * (1 + sources),
        out_specs=[pl.BlockSpec(memory_space=pltpu.VMEM)] * (sources // 2),
        out_shape=[jax.ShapeDtypeStruct(shape, F32 if i == 0 else BF16) for i in range(sources // 2)],
        scratch_shapes=[pltpu.VMEM((branches, states, states), F32), pltpu.VMEM((256, 256), BF16)],
        compiler_params=pltpu.CompilerParams(vmem_limit_bytes=32 << 20),
        cost_estimate=pl.CostEstimate(
            flops=4 * branches * states * states * width, bytes_accessed=4 * states * width, transcendentals=0
        ),
        name="products",
    )(x, *amps)


def iota(shape, dim):
    return lax.broadcasted_iota(jnp.int32, shape, dim)


def spread_kernel(_, out_ref):
    _, rows, lanes = out_ref.shape
    row, lane = iota((rows, lanes), 0), iota((rows, lanes), 1)
    here = row % (rows // 4) == lane // BANDS
    index = row // (rows // 4)
    out_ref[0] = (here & (index == lane % 4)).astype(F32).astype(BF16)
    out_ref[1] = (here & (index == lane % BANDS // 4)).astype(F32).astype(BF16)


def spread_matrices(size, earlier):
    return pl.pallas_call(
        spread_kernel,
        in_specs=[pl.BlockSpec(memory_space=pl.ANY)],
        out_specs=pl.BlockSpec(memory_space=pltpu.VMEM),
        out_shape=jax.ShapeDtypeStruct((2, 4 * size, size * BANDS), BF16),
        compiler_params=pltpu.CompilerParams(vmem_limit_bytes=24 << 20),
        cost_estimate=SMALL,
        name="spread",
    )(earlier)


def band_kernel(block_lines, lines_all, kq_ref, spread, coupling_ref, other_ref, next_ref, x_ref):
    branches, _, count = other_ref.shape
    half = BANDS // 4
    size = spread.shape[1] // 4
    shape = (8 * BANDS, 32)
    row, col = iota(shape, 0), iota(shape, 1)
    term, v, c = row // BANDS, row % BANDS // half, row % half
    choice = jnp.where(term < 4, 4 * term + c, 16 + 4 * v + (term - 4))
    pick = (choice == col).astype(F32).astype(BF16)
    shape = (branches * BANDS, size * BANDS)
    row, lane = iota(shape, 0) % BANDS, iota(shape, 1) % BANDS
    keep_cond = (row // half == lane // half).astype(F32)
    keep_val = (row % half == lane % half).astype(F32)
    _, _, core = place()
    base, _, _ = turns_of(kq_ref, core, block_lines, lines_all)
    late = jnp.where(base > 0, 1, 0)
    for part in range(2):
        block = part + late
        terms = []
        for branch in range(branches):
            table = jnp.where(block == core, coupling_ref[core, branch], other_ref[branch])
            table = jnp.where(block == 2, next_ref[branch], table)
            terms.append(contract(pick, table, 1, 0).astype(BF16))
        for start in range(0, count, size):
            width = min(size, count - start)
            lanes = width * BANDS
            values = []
            for kind in range(2):
                rows = []
                for term in terms:
                    slabs = []
                    for index in range(4):
                        at = (4 * kind + index) * BANDS
                        slab = term[at : at + BANDS, start : start + width]
                        if width < size:
                            slab = jnp.concatenate([slab, jnp.zeros((BANDS, size - width), BF16)], axis=1)
                        slabs.append(slab)
                    rows.append(jnp.concatenate(slabs, axis=1))
                values.append(contract(jnp.concatenate(rows, axis=0), spread[kind, :, :lanes], 1, 0))
            total = (values[0] * keep_cond[:, :lanes] - values[1] * keep_val[:, :lanes]).astype(BF16)
            at = (part * count + start) * BANDS
            for branch in range(branches):
                x_ref[branch, :, at : at + lanes] = total[branch * BANDS : (branch + 1) * BANDS]


def band_matrices(kq_map, spread, coupling, other, following, lines_all):
    branches, _, count = other.shape
    return pl.pallas_call(
        functools.partial(band_kernel, count // KY, lines_all),
        in_specs=[pl.BlockSpec(memory_space=pltpu.SMEM)] + [pl.BlockSpec(memory_space=pltpu.VMEM)] * 4,
        out_specs=pl.BlockSpec(memory_space=pltpu.VMEM),
        out_shape=jax.ShapeDtypeStruct((branches, BANDS, 2 * count * BANDS), BF16),
        compiler_params=pltpu.CompilerParams(vmem_limit_bytes=32 << 20),
        cost_estimate=SMALL,
        name="band_matrices",
    )(kq_map, spread, coupling, other, following)


def shards(envelopes, coupling, kq_map):
    n_pb, n_ka = lax.axis_size("pb"), lax.axis_size("ka")
    assert n_pb == 4 and n_ka % 2 == 0 and coupling.shape[0] == 2
    n_z = n_ka // 2
    rows, width = envelopes.shape
    block = width // n_ka
    lines_all = width // LINE
    branches = coupling.shape[1]
    core = lax.axis_index("ka") % 2

    def permute(x, to):
        pairs = []
        for p in range(n_pb):
            for k in range(n_ka):
                tp, tz, tc = to(p, k // 2, k % 2)
                pairs.append((p * n_ka + k, tp * n_ka + (tz % n_z) * 2 + tc))
        return lax.ppermute(x, ("pb", "ka"), pairs)

    def sibling(x):
        return permute(x, lambda p, zz, c: (p, zz, 1 - c))

    def passed_down(e):
        return lambda x: permute(x, lambda p, zz, c: (p, zz - e, c))

    def passed_down(x, e):
        return permute(x, lambda p, zz, c: (p, zz - e, c))

    def prepared(ins, for_other, direct=False):
        return prepare(kq_map, ins, block, lines_all, for_other, direct)

    def after(x, *others):
        return lax.optimization_barrier((x, *others))[0]

    near = sorted({1, n_z - 1})
    far = [e for e in range(2, n_z - 1)]
    *pieces, window, give = cut(envelopes, coupling, n_z, block)
    arrived = {e: passed_down(pieces[e - 1], e) for e in near}
    pass_on = prepared([window], True)
    keep = prepared([after(window, pass_on)], False)
    for e in far:
        arrived[e] = passed_down(after(pieces[e - 1], keep), e)
    spread = spread_matrices(min(coupling.shape[3], 64), keep)
    amps = {0: (keep, sibling(pass_on))}

    other_table = sibling(give)
    first_table = jnp.where(core == 0, lax.dynamic_index_in_dim(coupling, core, 0, keepdims=False), other_table)
    next_table = passed_down(first_table, 1)

    parts, first_steps = {}, []
    for e in near:
        piece = arrived[e]
        one = permute(piece, lambda p, zz, c: (p ^ (1 + c), zz, c))
        two = permute(piece, lambda p, zz, c: (p ^ (2 - c), zz, c))
        if e == 1:
            one = after(one, next_table)
        three = permute(one, lambda p, zz, c: (p ^ (2 - c), zz, c))
        first_steps += [one, two]
        parts[e] = [piece, one, two, three]
    for e in far:
        piece = after(arrived[e], next_table, *first_steps)
        parts[e] = [piece] + [permute(piece, lambda p, zz, c: (p ^ i, zz, c)) for i in (1, 2, 3)]
    x = band_matrices(kq_map, spread, coupling, other_table, after(next_table, *[parts[e][0] for e in far]), lines_all)
    for e in near + far:
        piece, *others = parts[e]
        done = [x] if e in near else [x, amps[1][0]]
        pass_on = prepared([after(piece, *done)] + others, True, e in far)
        keep = prepared([after(piece, pass_on)] + others, False, e in far)
        amps[e] = (keep, sibling(pass_on))
    amps = [half for e in range(n_z) for half in amps[e]]

    factor = 1.0 / math.sqrt(float(width))
    edges = [0] + [edge * branches // 9 for edge in GROUPS] + [branches]
    received, mine, other = [], [], []
    for lo, hi in zip(edges[:-1], edges[1:]):
        if len(received) >= 2:
            x, received[-2] = lax.optimization_barrier((x, received[-2]))
        own, *sends = products(x, amps, lo, hi - lo, factor)
        x, own = lax.optimization_barrier((x, own))
        if received:
            own, received[-1] = lax.optimization_barrier((own, received[-1]))
        received.append([own] + [permute(p, lambda p, zz, c: (p, zz + e, c)) for e, p in enumerate(sends, 1)])
    for parts in received:
        total = parts[0]
        for part in parts[1:]:
            total = total + part.astype(F32)
        mine.append(total[:, :rows])
        other.append(sibling(total[:, rows:]))
    mine, other = jnp.concatenate(mine, axis=0), jnp.concatenate(other, axis=0)
    return jnp.where(core == 0, jnp.stack([mine, other]), jnp.stack([other, mine]))


def solution(mesh):
    return jax.shard_map(
        shards,
        mesh=mesh,
        in_specs=(P("ka", None), P("pb", None, None, "ka"), P("pb", "ka")),
        out_specs=P("pb", None, "ka", None),
        check_vma=False,
    )
```

```python
import functools
import math

import jax
import jax.numpy as jnp
from jax import lax
from jax.experimental import pallas as pl
from jax.experimental.pallas import tpu as pltpu
from jax.sharding import PartitionSpec as P

KY = 96
BANDS = 16
LINE = KY * BANDS
GROUPS = (4, 8)
F32 = jnp.float32
SMALL = pl.CostEstimate(flops=1, bytes_accessed=1, transcendentals=0)
BF16 = jnp.bfloat16


def contract(a, b, dim_a, dim_b):
    return lax.dot_general(a, b, (((dim_a,), (dim_b,)), ((), ())), preferred_element_type=F32)


def place():
    ka = lax.axis_index("ka")
    return lax.axis_index("pb"), ka // 2, ka % 2


def turns_of(kq_ref, q, block_lines, lines_all):
    _, z, core = place()
    origin = kq_ref[q, 0]
    step = lax.rem(origin // KY - (2 * z + core) * block_lines + block_lines + lines_all, lines_all) - block_lines
    base = jnp.where(step < 0, block_lines, 0)
    return base, base + step, lax.rem(LINE - lax.rem(origin, KY) * BANDS, LINE)


def cut_kernel(block, n_z, sources, env_ref, coupling_ref, *refs):
    outs, sems = refs[:-1], refs[-1]
    pb, z, core = place()
    part = block // 4

    def lanes(chip, index):
        return pl.ds(pl.multiple_of(lax.rem(8 * chip + index, 8 * n_z) * part, 128), part)

    jobs = []
    for e, out in zip(sources, outs):
        to = lax.rem(z - e + n_z, n_z)
        for i in range(3):
            jobs.append((env_ref.at[:, lanes(to, 3 * pb + i)], out.at[:, i * part : (i + 1) * part]))
    if len(outs) > len(sources):
        window, give = outs[-2:]
        for i in range(12):
            jobs.append((env_ref.at[:, lanes(z, i)], window.at[:, i * part : (i + 1) * part]))
        jobs.append((coupling_ref.at[1 - core], give))
    copies = [pltpu.make_async_copy(src, dst, sems.at[i]) for i, (src, dst) in enumerate(jobs)]
    for copy in copies:
        copy.start()
    for copy in copies:
        copy.wait()


def cut(envelopes, coupling, n_z, block, sources, own):
    rows = envelopes.shape[0]
    shape = functools.partial(jax.ShapeDtypeStruct, dtype=BF16)
    outs = [shape((rows, 3 * block // 4))] * len(sources)
    if own:
        outs += [shape((rows, 3 * block)), shape(coupling.shape[1:])]
    return pl.pallas_call(
        functools.partial(cut_kernel, block, n_z, sources),
        in_specs=[pl.BlockSpec(memory_space=pl.ANY)] * 2,
        out_specs=[pl.BlockSpec(memory_space=pltpu.VMEM)] * len(outs),
        out_shape=outs,
        scratch_shapes=[pltpu.SemaphoreType.DMA((3 * len(sources) + 13,))],
        cost_estimate=SMALL,
        name="cut_own" if own else "cut",
    )(envelopes, coupling)


def prep_kernel(block_lines, lines_all, for_other, direct, kq_ref, *refs):
    ins, (out_ref, window) = refs[:-2], refs[-2:]
    pb, _, core = place()
    q = 1 - core if for_other else core
    base, image, turn = turns_of(kq_ref, q, block_lines, lines_all)
    if len(ins) == 1:
        window = ins[0]
    else:
        for rel, src in zip((0, 1, 2, 3) if direct else (0, 1 + core, 2 - core, 3), ins):
            size = src.shape[1]
            window[:, pl.ds(pl.multiple_of((pb ^ rel) * size, 128), size)] = src[...]
    for line in range(2 * block_lines):
        to = slice(line * LINE, (line + 1) * LINE)
        out_ref[0, :, to] = window[:, pl.ds(pl.multiple_of((base + line) * LINE, 128), LINE)]
        shifted = window[:, pl.ds(pl.multiple_of((image + line) * LINE, 128), LINE)].astype(F32)
        out_ref[1, :, to] = pltpu.roll(shifted, turn, 1).astype(BF16)


def prepare(kq_map, ins, block, lines_all, for_other, direct):
    rows = ins[0].shape[0]
    return pl.pallas_call(
        functools.partial(prep_kernel, block // LINE, lines_all, for_other, direct),
        in_specs=[pl.BlockSpec(memory_space=pltpu.SMEM)] + [pl.BlockSpec(memory_space=pltpu.VMEM)] * len(ins),
        out_specs=pl.BlockSpec(memory_space=pltpu.VMEM),
        out_shape=jax.ShapeDtypeStruct((2, rows, 2 * block), BF16),
        scratch_shapes=[pltpu.VMEM((rows, 3 * block), BF16)],
        compiler_params=pltpu.CompilerParams(vmem_limit_bytes=16 << 20),
        cost_estimate=SMALL,
        name="prepare_other" if for_other else "prepare_own",
    )(kq_map, *ins)


def main_kernel(sources, first, branches, factor, x_ref, *refs):
    amps, (mine_ref, *sends, total, mask) = refs[:sources], refs[sources:]
    shape = mask.shape
    same = lax.broadcasted_iota(jnp.int32, shape, 0) // BANDS == lax.broadcasted_iota(jnp.int32, shape, 1) // BANDS
    mask[...] = same.astype(F32).astype(BF16)
    for line in range(x_ref.shape[2] // LINE):
        to = slice(line * LINE, (line + 1) * LINE)
        for branch in range(branches):
            parts = []
            for tile in range(LINE // 256):
                lanes = slice(line * LINE + tile * 256, line * LINE + (tile + 1) * 256)
                matrix = jnp.concatenate([x_ref[first + branch, :, lanes]] * 16, axis=0) * mask[...]
                own = jnp.concatenate([ref[0, :, lanes] for ref in amps], axis=0)
                parts.append(contract(own, matrix, 1, 0).astype(BF16))
            shifted = jnp.concatenate([ref[1, :, to] for ref in amps], axis=0)
            part = contract(shifted, jnp.concatenate(parts, axis=1), 1, 1)
            total[branch] = part if line == 0 else total[branch] + part
    _, z, core = place()
    states = total.shape[2]
    rows = states // sources
    col = lax.broadcasted_iota(jnp.int32, (states, states), 0)
    target = lax.broadcasted_iota(jnp.int32, (states, states), 1)
    source = lax.rem(col // rows + 2 * z, sources)
    home = (source // 2 * 2 + (source % 2 ^ core)) * rows + col % rows
    to_home = (home == target).astype(F32).astype(BF16)
    for branch in range(branches):
        value = total[branch] * factor
        high = value.astype(BF16)
        moved = contract(high, to_home, 1, 0)
        rest = value[: 2 * rows] - high[: 2 * rows].astype(F32)
        middle = rest.astype(BF16)
        low = (rest - middle.astype(F32)).astype(BF16)
        mine_ref[branch] = moved[: 2 * rows] + contract(middle, to_home, 1, 0) + contract(low, to_home, 1, 0)
        for chip, send in enumerate(sends, 1):
            send[branch] = moved[chip * 2 * rows : (chip + 1) * 2 * rows].astype(BF16)


def products(x, amps, first, branches, factor):
    sources, rows = len(amps), amps[0].shape[1]
    states, width = sources * rows, x.shape[2]
    shape = (branches, 2 * rows, states)
    return pl.pallas_call(
        functools.partial(main_kernel, sources, first, branches, factor),
        in_specs=[pl.BlockSpec(memory_space=pltpu.VMEM)] * (1 + sources),
        out_specs=[pl.BlockSpec(memory_space=pltpu.VMEM)] * (sources // 2),
        out_shape=[jax.ShapeDtypeStruct(shape, F32 if i == 0 else BF16) for i in range(sources // 2)],
        scratch_shapes=[pltpu.VMEM((branches, states, states), F32), pltpu.VMEM((256, 256), BF16)],
        compiler_params=pltpu.CompilerParams(vmem_limit_bytes=32 << 20),
        cost_estimate=pl.CostEstimate(
            flops=4 * branches * states * states * width, bytes_accessed=4 * states * width, transcendentals=0
        ),
        name="products",
    )(x, *amps)


def iota(shape, dim):
    return lax.broadcasted_iota(jnp.int32, shape, dim)


def spread_kernel(_, out_ref):
    _, rows, lanes = out_ref.shape
    row, lane = iota((rows, lanes), 0), iota((rows, lanes), 1)
    here = row % (rows // 4) == lane // BANDS
    index = row // (rows // 4)
    out_ref[0] = (here & (index == lane % 4)).astype(F32).astype(BF16)
    out_ref[1] = (here & (index == lane % BANDS // 4)).astype(F32).astype(BF16)


def spread_matrices(size, earlier):
    return pl.pallas_call(
        spread_kernel,
        in_specs=[pl.BlockSpec(memory_space=pl.ANY)],
        out_specs=pl.BlockSpec(memory_space=pltpu.VMEM),
        out_shape=jax.ShapeDtypeStruct((2, 4 * size, size * BANDS), BF16),
        compiler_params=pltpu.CompilerParams(vmem_limit_bytes=24 << 20),
        cost_estimate=SMALL,
        name="spread",
    )(earlier)


def band_kernel(block_lines, lines_all, kq_ref, spread, coupling_ref, other_ref, next_ref, x_ref):
    branches, _, count = other_ref.shape
    half = BANDS // 4
    size = spread.shape[1] // 4
    shape = (8 * BANDS, 32)
    row, col = iota(shape, 0), iota(shape, 1)
    term, v, c = row // BANDS, row % BANDS // half, row % half
    choice = jnp.where(term < 4, 4 * term + c, 16 + 4 * v + (term - 4))
    pick = (choice == col).astype(F32).astype(BF16)
    shape = (branches * BANDS, size * BANDS)
    row, lane = iota(shape, 0) % BANDS, iota(shape, 1) % BANDS
    keep_cond = (row // half == lane // half).astype(F32)
    keep_val = (row % half == lane % half).astype(F32)
    _, _, core = place()
    base, _, _ = turns_of(kq_ref, core, block_lines, lines_all)
    late = jnp.where(base > 0, 1, 0)
    for part in range(2):
        block = part + late
        terms = []
        for branch in range(branches):
            table = jnp.where(block == core, coupling_ref[core, branch], other_ref[branch])
            table = jnp.where(block == 2, next_ref[branch], table)
            terms.append(contract(pick, table, 1, 0).astype(BF16))
        for start in range(0, count, size):
            width = min(size, count - start)
            lanes = width * BANDS
            values = []
            for kind in range(2):
                rows = []
                for term in terms:
                    slabs = []
                    for index in range(4):
                        at = (4 * kind + index) * BANDS
                        slab = term[at : at + BANDS, start : start + width]
                        if width < size:
                            slab = jnp.concatenate([slab, jnp.zeros((BANDS, size - width), BF16)], axis=1)
                        slabs.append(slab)
                    rows.append(jnp.concatenate(slabs, axis=1))
                values.append(contract(jnp.concatenate(rows, axis=0), spread[kind, :, :lanes], 1, 0))
            total = (values[0] * keep_cond[:, :lanes] - values[1] * keep_val[:, :lanes]).astype(BF16)
            at = (part * count + start) * BANDS
            for branch in range(branches):
                x_ref[branch, :, at : at + lanes] = total[branch * BANDS : (branch + 1) * BANDS]


def band_matrices(kq_map, spread, coupling, other, following, lines_all):
    branches, _, count = other.shape
    return pl.pallas_call(
        functools.partial(band_kernel, count // KY, lines_all),
        in_specs=[pl.BlockSpec(memory_space=pltpu.SMEM)] + [pl.BlockSpec(memory_space=pltpu.VMEM)] * 4,
        out_specs=pl.BlockSpec(memory_space=pltpu.VMEM),
        out_shape=jax.ShapeDtypeStruct((branches, BANDS, 2 * count * BANDS), BF16),
        compiler_params=pltpu.CompilerParams(vmem_limit_bytes=32 << 20),
        cost_estimate=SMALL,
        name="band_matrices",
    )(kq_map, spread, coupling, other, following)


def shards(envelopes, coupling, kq_map):
    n_pb, n_ka = lax.axis_size("pb"), lax.axis_size("ka")
    assert n_pb == 4 and n_ka % 2 == 0 and coupling.shape[0] == 2
    n_z = n_ka // 2
    rows, width = envelopes.shape
    block = width // n_ka
    lines_all = width // LINE
    branches = coupling.shape[1]
    core = lax.axis_index("ka") % 2

    def permute(x, to):
        pairs = []
        for p in range(n_pb):
            for k in range(n_ka):
                tp, tz, tc = to(p, k // 2, k % 2)
                pairs.append((p * n_ka + k, tp * n_ka + (tz % n_z) * 2 + tc))
        return lax.ppermute(x, ("pb", "ka"), pairs)

    def sibling(x):
        return permute(x, lambda p, zz, c: (p, zz, 1 - c))

    def passed_down(e):
        return lambda x: permute(x, lambda p, zz, c: (p, zz - e, c))

    def passed_down(x, e):
        return permute(x, lambda p, zz, c: (p, zz - e, c))

    def prepared(ins, for_other, direct=False):
        return prepare(kq_map, ins, block, lines_all, for_other, direct)

    def after(x, *others):
        return lax.optimization_barrier((x, *others))[0]

    near = sorted({1, n_z - 1})
    far = [e for e in range(2, n_z - 1)]
    first = cut(envelopes, coupling, n_z, block, near, False)
    arrived = {e: passed_down(piece, e) for e, piece in zip(near, first)}
    *later, window, give = cut(after(envelopes, first[0]), coupling, n_z, block, far, True)
    pieces = dict(zip(far, later))
    pass_on = prepared([window], True)
    keep = prepared([after(window, pass_on)], False)
    for e in far:
        arrived[e] = passed_down(after(pieces[e], keep), e)
    spread = spread_matrices(min(coupling.shape[3], 64), keep)
    amps = {0: (keep, sibling(pass_on))}

    other_table = sibling(give)
    first_table = jnp.where(core == 0, lax.dynamic_index_in_dim(coupling, core, 0, keepdims=False), other_table)
    next_table = passed_down(first_table, 1)

    parts, first_steps = {}, []
    for e in near:
        piece = arrived[e]
        one = permute(piece, lambda p, zz, c: (p ^ (1 + c), zz, c))
        two = permute(piece, lambda p, zz, c: (p ^ (2 - c), zz, c))
        if e == 1:
            one = after(one, next_table)
        three = permute(one, lambda p, zz, c: (p ^ (2 - c), zz, c))
        first_steps += [one, two, three] if e == 1 else [one, two]
        parts[e] = [piece, one, two, three]
    x = band_matrices(kq_map, spread, coupling, other_table, next_table, lines_all)
    for e in far:
        piece = after(arrived[e], x, *first_steps)
        parts[e] = [piece] + [permute(piece, lambda p, zz, c: (p ^ i, zz, c)) for i in (1, 2, 3)]
    for e in near + far:
        piece, *others = parts[e]
        done = [parts[far[0]][0]] if e in near else [amps[1][0]]
        pass_on = prepared([after(piece, *done)] + others, True, e in far)
        keep = prepared([after(piece, pass_on)] + others, False, e in far)
        amps[e] = (keep, sibling(pass_on))
    amps = [half for e in range(n_z) for half in amps[e]]

    factor = 1.0 / math.sqrt(float(width))
    edges = [0] + [edge * branches // 9 for edge in GROUPS] + [branches]
    received, mine, other = [], [], []
    for lo, hi in zip(edges[:-1], edges[1:]):
        if len(received) >= 2:
            x, received[-2] = lax.optimization_barrier((x, received[-2]))
        own, *sends = products(x, amps, lo, hi - lo, factor)
        x, own = lax.optimization_barrier((x, own))
        if received:
            own, received[-1] = lax.optimization_barrier((own, received[-1]))
        received.append([own] + [permute(p, lambda p, zz, c: (p, zz + e, c)) for e, p in enumerate(sends, 1)])
    totals = []
    for parts in received:
        total = parts[0]
        for part in parts[1:]:
            total = total + part.astype(F32)
        totals.append(total)
    for total in totals[:-2] + [jnp.concatenate(totals[-2:], axis=0)]:
        mine.append(total[:, :rows])
        other.append(sibling(total[:, rows:]))
    mine, other = jnp.concatenate(mine, axis=0), jnp.concatenate(other, axis=0)
    return jnp.where(core == 0, jnp.stack([mine, other]), jnp.stack([other, mine]))


def solution(mesh):
    return jax.shard_map(
        shards,
        mesh=mesh,
        in_specs=(P("ka", None), P("pb", None, None, "ka"), P("pb", "ka")),
        out_specs=P("pb", None, "ka", None),
        check_vma=False,
    )
```
